32 devices in a mesh: seq: 8 (over y, x, core), fsdp: 4 (over z).
Axes of the slice: x: 2, y: 2, z: 4, core: 2. Of those that a mesh axis runs over, the one named last changes fastest.
Arguments:
- hidden_in: bfloat16 [4, 1024, 2048], P('fsdp', 'seq'), may hold values from -6 to 6
- positions: int32 [4, 1024], P('fsdp'), may hold values from 0 to 1535, as said below
- norm1_gain: bfloat16 [2048], P(('seq', 'fsdp')), may hold values from 0.25 to 1.75
- norm1_shift: bfloat16 [2048], P(('seq', 'fsdp')), may hold values from -3 to 3
- w_qkv: bfloat16 [2048, 6144], P(('seq', 'fsdp')), may hold values from -0.125 to 0.125
- b_qkv: bfloat16 [6144], P(('seq', 'fsdp')), may hold values from -3 to 3
- w_out: bfloat16 [2048, 2048], P(('seq', 'fsdp')), may hold values from -4 to 4
- norm2_gain: bfloat16 [2048], P(('seq', 'fsdp')), may hold values from 0.25 to 1.75
- norm2_shift: bfloat16 [2048], P(('seq', 'fsdp')), may hold values from -3 to 3
- w_gate: bfloat16 [2048, 5632], P(('seq', 'fsdp')), may hold values from -0.125 to 0.125
- w_up: bfloat16 [2048, 5632], P(('seq', 'fsdp')), may hold values from -0.125 to 0.125
- w_down: bfloat16 [5632, 2048], P(('seq', 'fsdp')), may hold values from -0.078125 to 0.078125
- grad_out: bfloat16 [4, 1024, 2048], P('fsdp', 'seq'), may hold values from -6 to 6
Outputs:
- layer_out: bfloat16 [4, 1024, 2048], P('fsdp', 'seq')
- grad_in: bfloat16 [4, 1024, 2048], P('fsdp', 'seq')
- grad_norm1_gain: float32 [2048], P(('seq', 'fsdp'))
- grad_norm1_shift: float32 [2048], P(('seq', 'fsdp'))
- grad_w_qkv: float32 [2048, 6144], P(('seq', 'fsdp'))
- grad_b_qkv: float32 [6144], P(('seq', 'fsdp'))
- grad_w_out: float32 [2048, 2048], P(('seq', 'fsdp'))
- grad_norm2_gain: float32 [2048], P(('seq', 'fsdp'))
- grad_norm2_shift: float32 [2048], P(('seq', 'fsdp'))
- grad_w_gate: float32 [2048, 5632], P(('seq', 'fsdp'))
- grad_w_up: float32 [2048, 5632], P(('seq', 'fsdp'))
- grad_w_down: float32 [5632, 2048], P(('seq', 'fsdp'))
The draws below stay inside these ranges and needn't reach their ends.
Inputs may be any that keep to these rules, and one draw needn't show every extreme that they name: In every sequence, positions start at 0 and rise strictly by steps of 1 or 2, and the last one is 1535.
All inputs are finite; a program needn't handle non-finite values.
Results may differ from the reference program's by a relative error of at most 0.012.
Values may be sent and summed in bfloat16 or wider, within the bound.
No kernel may reach another device: no remote copies, remote signals or barrier semaphores. Data moves between devices by JAX's collectives and lax.ppermute only.
A program may use at most 512 MiB of HBM per device.

```python
import jax
import jax.numpy as jnp
from jax import lax

D = 2048
H = 32
HD = 64
FF = 5632
ROT = 16
LENGTH = 1024
SEQS = 4
TOKENS = 4096


def draw_positions(key, part):
    key = jax.random.fold_in(key, 7)
    seq_keys = jax.random.split(key, SEQS)

    def one_sequence(seq_key):
        order = jax.random.permutation(seq_key, LENGTH - 1)
        steps_up = 1 + (order < LENGTH // 2).astype(jnp.int32)
        return jnp.concatenate([jnp.zeros((1,), jnp.int32), jnp.cumsum(steps_up).astype(jnp.int32)])
    return jax.vmap(one_sequence)(seq_keys)


def block_scale(rng, extent, cuts, low, high):
    factor_of, own = 1.0, jax.random.fold_in(rng, 6)
    for axis_at, parts in cuts:
        steps = jnp.exp(jax.random.uniform(jax.random.fold_in(own, axis_at), (parts,), jnp.float32, low / len(cuts), high / len(cuts)))
        factor_of = factor_of * jnp.repeat(steps, extent[axis_at] // parts).reshape([-1 if axis == axis_at else 1 for axis in range(len(extent))])
    return factor_of


def normal_values(key, dims, scale, limit, shards=(), held_as=jnp.bfloat16):
    loudness = block_scale(key, dims, shards, -0.22, 0.18) if shards else 1.0
    values = jax.random.normal(key, dims, jnp.float32) * scale * loudness
    return jnp.minimum(jnp.maximum(values, -limit), limit).astype(held_as)


def setup_inputs(seed: int = 0) -> dict:
    arg_keys = jax.random.split(jax.random.key(seed), 14)
    return {
        "hidden_in": normal_values(arg_keys[0], (SEQS, LENGTH, D), 1.0, 6.0, ((0, 4), (1, 8))),
        "positions": draw_positions(jax.random.fold_in(arg_keys[13], 71), 0),
        "norm1_gain": jnp.clip(1.0 + 0.15 * jax.random.normal(arg_keys[2], (D,), jnp.float32), 0.25, 1.75).astype(jnp.bfloat16),
        "norm1_shift": normal_values(arg_keys[3], (D,), 0.5, 3.0, ((0, 32),)),
        "w_qkv": normal_values(arg_keys[4], (D, 3 * D), D ** -0.5, 0.125, ((0, 32),)),
        "b_qkv": normal_values(arg_keys[5], (3 * D,), 0.5, 3.0, ((0, 32),)),
        "w_out": normal_values(arg_keys[6], (D, D), (max(1, D // 1024)) ** -0.5, 4.0, ((0, 32),)),
        "norm2_gain": jnp.clip(1.0 + 0.15 * jax.random.normal(arg_keys[7], (D,), jnp.float32), 0.25, 1.75).astype(jnp.bfloat16),
        "norm2_shift": normal_values(arg_keys[8], (D,), 0.5, 3.0, ((0, 32),)),
        "w_gate": normal_values(arg_keys[9], (D, FF), D ** -0.5, 0.125, ((0, 32),)),
        "w_up": normal_values(arg_keys[10], (D, FF), D ** -0.5, 0.125, ((0, 32),)),
        "w_down": normal_values(arg_keys[11], (FF, D), FF ** -0.5, 0.078125, ((0, 32),)),
        "grad_out": normal_values(arg_keys[12], (SEQS, LENGTH, D), 1.0, 6.0, ((0, 4), (1, 8))),
    }


@jax.custom_vjp
def low(v):
    return lax.optimization_barrier(v.astype(jnp.bfloat16)).astype(jnp.float32)

@jax.custom_vjp
def low_back(v):
    return v

def low_keep(v):
    return (low(v), None)

def low_pass(kept, grad):
    return (grad,)

def back_keep(v):
    return (v, None)

def back_low(kept, grad):
    return (low(grad),)
low.defvjp(low_keep, low_pass)
low_back.defvjp(back_keep, back_low)
EPS = 1e-05
NEG = -1e+30
HIGH = lax.Precision.HIGHEST

def layer_norm(values, gain_row, shift_row):
    row_mean = lax.optimization_barrier(jnp.mean(values, axis=1, keepdims=True))
    centred = values - row_mean
    inverse = lax.rsqrt(lax.optimization_barrier(jnp.mean(centred * centred, axis=1, keepdims=True)) + EPS)
    return centred * inverse * gain_row + shift_row

def angle_tables(positions_here):
    half_rot = ROT // 2
    frequency = 10000.0 ** (-2.0 * jnp.arange(half_rot, dtype=jnp.float32) / ROT)
    angles = positions_here.astype(jnp.float32)[:, None] * frequency[None, :]
    return (jnp.concatenate([jnp.cos(angles), jnp.cos(angles)], 1), jnp.concatenate([jnp.sin(angles), jnp.sin(angles)], 1))

def rotate(head_view, cosine_table, sine_table):
    half_rot = ROT // 2
    turning = head_view[:, :, :ROT]
    swapped = jnp.concatenate([-turning[:, :, half_rot:], turning[:, :, :half_rot]], 2)
    turned = turning * cosine_table[:, None, :] + swapped * sine_table[:, None, :]
    return jnp.concatenate([turned, head_view[:, :, ROT:]], 2)

def attention(queries, key_rows, values, positions):
    block_len = min(LENGTH, 2048)
    block_count = LENGTH // block_len
    score_scale = HD ** (-0.5)

    def by_heads(array):
        return jnp.transpose(array.reshape(SEQS, LENGTH, H, HD), (0, 2, 1, 3))
    query_seqs = by_heads(queries).reshape(SEQS, H, block_count, block_len, HD)
    key_seqs = by_heads(key_rows)
    value_seqs = by_heads(values)

    def one_sequence(seq_args):
        q_seq, k_seq, v_seq, places = seq_args
        query_places = places.reshape(block_count, block_len)

        def one_head(head_args):
            q_head, k_head, v_head = head_args

            def one_block(block_args):
                q_block, q_places = block_args
                scores = low_back(jnp.einsum('qd,kd->qk', q_block, k_head, precision=HIGH) * score_scale)
                allowed = places[None, :] <= q_places[:, None]
                scores = jnp.where(allowed, scores, NEG)
                row_peak = lax.optimization_barrier(jnp.max(scores, axis=1, keepdims=True))
                exp_scores = jnp.exp(scores - row_peak)
                soft_weights = low(exp_scores / lax.optimization_barrier(jnp.sum(exp_scores, axis=1, keepdims=True)))
                return low(low_back(jnp.dot(soft_weights, v_head, precision=HIGH)))
            return lax.map(jax.checkpoint(one_block), (q_head, query_places))
        return lax.map(jax.checkpoint(one_head), (q_seq, k_seq, v_seq))
    attended = lax.map(one_sequence, (query_seqs, key_seqs, value_seqs, positions))
    attended = attended.reshape(SEQS, H, LENGTH, HD)
    return jnp.transpose(attended, (0, 2, 1, 3)).reshape(TOKENS, D)

def layer(inputs, first_gain, first_shift, qkv_weight, qkv_bias, out_weight, second_gain, second_shift, gate_weight, up_weight, down_weight, cosine_table, sine_table, positions):
    rows_in = inputs.reshape(TOKENS, D)
    first_normed = low(layer_norm(rows_in, first_gain, first_shift))
    projected = low_back(jnp.dot(first_normed, qkv_weight, precision=HIGH) + qkv_bias)
    queries = low(low_back(rotate(projected[:, :D].reshape(TOKENS, H, HD), cosine_table, sine_table)))
    key_rows = low(low_back(rotate(projected[:, D:2 * D].reshape(TOKENS, H, HD), cosine_table, sine_table)))
    values = low(low_back(projected[:, 2 * D:].reshape(TOKENS, H, HD)))
    mixed_rows = attention(queries, key_rows, values, positions)
    middle = rows_in + low_back(jnp.dot(mixed_rows, out_weight, precision=HIGH))
    second_normed = low(layer_norm(middle, second_gain, second_shift))
    gate_act = low_back(jnp.dot(second_normed, gate_weight, precision=HIGH))
    up_act = low_back(jnp.dot(second_normed, up_weight, precision=HIGH))
    hidden_mid = low(gate_act / (1.0 + jnp.exp(-gate_act)) * up_act)
    result = middle + low_back(jnp.dot(hidden_mid, down_weight, precision=HIGH))
    return result.reshape(SEQS, LENGTH, D)

def reference(hidden_in, positions, norm1_gain, norm1_shift, w_qkv, b_qkv, w_out, norm2_gain, norm2_shift, w_gate, w_up, w_down, grad_out):
    cosine_table, sine_table = angle_tables(positions.reshape(TOKENS))

    def forward(inputs, first_gain, first_shift, qkv_weight, qkv_bias, out_weight, second_gain, second_shift, gate_weight, up_weight, down_weight):
        return layer(inputs, first_gain, first_shift, qkv_weight, qkv_bias, out_weight, second_gain, second_shift, gate_weight, up_weight, down_weight, cosine_table, sine_table, positions)
    layer_out, pullback = jax.vjp(forward, hidden_in.astype(jnp.float32), norm1_gain.astype(jnp.float32), norm1_shift.astype(jnp.float32), w_qkv.astype(jnp.float32), b_qkv.astype(jnp.float32), w_out.astype(jnp.float32), norm2_gain.astype(jnp.float32), norm2_shift.astype(jnp.float32), w_gate.astype(jnp.float32), w_up.astype(jnp.float32), w_down.astype(jnp.float32))
    gradients = pullback(grad_out.astype(jnp.float32))
    return (layer_out.astype(jnp.bfloat16), gradients[0].astype(jnp.bfloat16), gradients[1], gradients[2], gradients[3], gradients[4], gradients[5], gradients[6], gradients[7], gradients[8], gradients[9], gradients[10])
```

```python
import jax
import jax.numpy as jnp
from jax import lax
from jax.sharding import PartitionSpec as P

HD = 64
ROT = 16

EPS = 1e-05
NEG = -1e30

BF = jnp.bfloat16
F4 = jnp.float32


def dot(a, b, out=F4):
    return jnp.dot(a, b, preferred_element_type=F4).astype(out)


def dot_nt(a, b):
    return lax.dot_general(a, b, (((1,), (1,)), ((), ())), preferred_element_type=F4)


def dot_tn(a, b):
    return lax.dot_general(a, b, (((0,), (0,)), ((), ())), preferred_element_type=F4)


def layer_norm(values, gain_row, shift_row):
    row_mean = jnp.mean(values, axis=1, keepdims=True)
    centred = values - row_mean
    inverse = lax.rsqrt(jnp.mean(centred * centred, axis=1, keepdims=True) + EPS)
    normed = centred * inverse
    return (normed * gain_row.astype(F4) + shift_row.astype(F4), normed, inverse)


def norm_backward(grad_rows, normed, inverse, gain_row):
    scaled = grad_rows * gain_row.astype(F4)
    inner_term = (
        scaled
        - jnp.mean(scaled, axis=1, keepdims=True)
        - normed * jnp.mean(scaled * normed, axis=1, keepdims=True)
    )
    return (inner_term * inverse, jnp.sum(grad_rows * normed, axis=0), jnp.sum(grad_rows, axis=0))


def angle_tables(places):
    half_rot = ROT // 2
    frequency = 10000.0 ** (-2.0 * jnp.arange(half_rot, dtype=F4) / ROT)
    angles = places.astype(F4)[:, None] * frequency[None, :]
    return (
        jnp.concatenate([jnp.cos(angles), jnp.cos(angles)], 1),
        jnp.concatenate([jnp.sin(angles), jnp.sin(angles)], 1),
    )


def rotate(flat_rows, cosine_table, sine_table, backward):
    row_count = flat_rows.shape[0]
    head_view = flat_rows.reshape(row_count, -1, HD)
    half_rot = ROT // 2
    turning = head_view[:, :, :ROT]
    if backward:
        swapped = jnp.concatenate([turning[:, :, half_rot:], -turning[:, :, :half_rot]], 2)
    else:
        swapped = jnp.concatenate([-turning[:, :, half_rot:], turning[:, :, :half_rot]], 2)
    turned = turning * cosine_table[:, None, :] + swapped * sine_table[:, None, :]
    return jnp.concatenate([turned, head_view[:, :, ROT:]], 2).reshape(row_count, -1)


def block_scores(query_part, key_part, query_place, key_place, score_scale):
    scores = (
        jnp.einsum("qhd,khd->hqk", query_part, key_part, preferred_element_type=F4) * score_scale
    )
    allowed = key_place[None, :] <= query_place[:, None]
    return jnp.where(allowed[None], scores, NEG)


def attend(query_heads, all_keys, all_values, places, score_scale):
    rows = places.shape[0]
    block_rows = min(512, rows)
    attended, log_totals = [], []
    for block_index in range(rows // block_rows):
        keys_len = (block_index + 1) * block_rows
        rows_now = slice(block_index * block_rows, keys_len)
        scores = block_scores(
            query_heads[rows_now], all_keys[:keys_len], places[rows_now], places[:keys_len], score_scale
        )
        row_peak = jnp.max(scores, axis=2, keepdims=True)
        exp_scores = jnp.exp(scores - row_peak)
        summed = jnp.sum(exp_scores, axis=2, keepdims=True)
        soft_weights = (exp_scores / summed).astype(BF)
        block_out = jnp.einsum(
            "hqk,khd->qhd", soft_weights, all_values[:keys_len], preferred_element_type=F4
        )
        attended.append(block_out.astype(BF))
        log_totals.append(row_peak[:, :, 0] + jnp.log(summed[:, :, 0]))
    return jnp.concatenate(attended, 0).reshape(rows, -1), log_totals


def attend_backward(query_heads, all_keys, all_values, grad_heads, log_totals, places, score_scale):
    rows = places.shape[0]
    cols = query_heads.shape[1] * HD
    block_rows = min(512, rows)
    key_grad = jnp.zeros((rows, cols), F4)
    value_grad = jnp.zeros((rows, cols), F4)
    query_terms = []
    for block_index in range(rows // block_rows):
        keys_len = (block_index + 1) * block_rows
        rows_now = slice(block_index * block_rows, keys_len)
        query_part = query_heads[rows_now]
        grad_part = grad_heads[rows_now]
        scores = block_scores(
            query_part, all_keys[:keys_len], places[rows_now], places[:keys_len], score_scale
        )
        probs_now = jnp.exp(scores - log_totals[block_index][:, :, None])
        d_probs = jnp.einsum(
            "qhd,khd->hqk", grad_part, all_values[:keys_len], preferred_element_type=F4
        )
        centre = jnp.sum(probs_now * d_probs, axis=2, keepdims=True)
        d_scores = (probs_now * (d_probs - centre)).astype(BF)
        d_values = jnp.einsum(
            "hqk,qhd->khd", probs_now.astype(BF), grad_part, preferred_element_type=F4
        )
        d_keys = (
            jnp.einsum("hqk,qhd->khd", d_scores, query_part, preferred_element_type=F4) * score_scale
        )
        d_queries = (
            jnp.einsum("hqk,khd->qhd", d_scores, all_keys[:keys_len], preferred_element_type=F4)
            * score_scale
        )
        query_terms.append(d_queries.astype(BF))
        key_grad = key_grad.at[:keys_len].add(d_keys.reshape(keys_len, cols))
        value_grad = value_grad.at[:keys_len].add(d_values.reshape(keys_len, cols))
    query_grad = jnp.concatenate(query_terms, 0).reshape(rows, cols)
    return query_grad, key_grad.astype(BF), value_grad.astype(BF)


class Links:
    def __init__(self):
        self.ns = lax.axis_size("seq")
        self.nz = lax.axis_size("fsdp")
        self.s = lax.axis_index("seq")
        self.z = lax.axis_index("fsdp")
        self.core = self.s % 2
        self.fast_plane = self.ns == 8
        self.fast_line = self.nz == 4
        self.order = [0, 2, 4, 6, 1, 3, 5, 7]

    def flip(self, values, bit):
        return lax.ppermute(values, "seq", [(i, i ^ bit) for i in range(self.ns)])

    def swap_core(self, values):
        return self.flip(values, 1)

    def hop(self, values, pairs):
        return lax.ppermute(values, "fsdp", pairs)

    def plane_gather(self, own):
        if not self.fast_plane:
            return lax.all_gather(own, "seq", axis=0, tiled=True)
        half = own.shape[0] // 2
        own_other = self.swap_core(own)
        along_x = self.flip(own, 2)
        along_y = self.flip(own, 4)
        far_a = self.flip(along_x[:half], 4)
        far_b = self.flip(along_y[half:], 2)
        rest = [self.swap_core(part) for part in (along_x, along_y, far_a, far_b)]
        return jnp.concatenate([own, along_x, along_y, far_a, far_b, own_other] + rest, 0)

    def plane_reduce(self, keep, send):
        if not self.fast_plane:
            return lax.psum_scatter(
                jnp.concatenate([keep, send], 0).astype(BF), "seq", scatter_dimension=0, tiled=True
            ).astype(F4)
        rows = keep.shape[0] // 4
        half = rows // 2
        pair = keep + self.swap_core(send.astype(BF)).astype(F4)
        own, to_x, to_y, far = (pair[i * rows : (i + 1) * rows] for i in range(4))
        far = far.astype(BF)
        via_x = self.flip(far[:half], 2)
        via_y = self.flip(far[half:], 4)
        to_y = jnp.concatenate([to_y[:half] + via_x.astype(F4), to_y[half:]], 0).astype(BF)
        to_x = jnp.concatenate([to_x[:half], to_x[half:] + via_y.astype(F4)], 0).astype(BF)
        from_x = self.flip(to_x, 2)
        from_y = self.flip(to_y, 4)
        return own + from_x.astype(F4) + from_y.astype(F4)

    def plane_sorted(self, rows_in):
        if not self.fast_plane:
            return rows_in
        chunk = rows_in.shape[0] // self.ns
        at = jnp.array([self.order.index(j) for j in range(8)], jnp.int32)
        parts = [
            lax.dynamic_slice_in_dim(rows_in, at[self.s ^ j] * chunk, chunk, 0) for j in range(8)
        ]
        return jnp.concatenate(parts, 0)

    def plane_unsorted(self, rows_in):
        if not self.fast_plane:
            return rows_in
        chunk = rows_in.shape[0] // self.ns
        parts = [
            lax.dynamic_slice_in_dim(rows_in, (self.s ^ k) * chunk, chunk, 0) for k in self.order
        ]
        return jnp.concatenate(parts, 0)

    def line_gather(self, own):
        if not self.fast_line:
            mine = lax.all_gather(own, "fsdp", axis=0, tiled=True)
            return jnp.concatenate([mine, self.swap_core(mine)], 0)
        up1 = self.hop(own, [(0, 1), (1, 2), (2, 3)])
        down1 = self.hop(own, [(3, 2), (2, 1), (1, 0)])
        up2 = self.hop(up1, [(1, 2), (2, 3)])
        down2 = self.hop(down1, [(2, 1), (1, 0)])
        up3 = self.hop(up2, [(2, 3)])
        down3 = self.hop(down2, [(1, 0)])
        parts = [
            own,
            jnp.where(self.z >= 1, up1, down3),
            jnp.where(self.z >= 2, up2, down2),
            jnp.where(self.z >= 3, up3, down1),
        ]
        return jnp.concatenate(parts + [self.swap_core(part) for part in parts], 0)

    def line_reduce(self, keep, send):
        pair = keep + self.swap_core(send.astype(BF)).astype(F4)
        if not self.fast_line:
            return lax.psum_scatter(pair.astype(BF), "fsdp", scatter_dimension=0, tiled=True).astype(F4)
        rows = pair.shape[0] // 4
        own, one, two, three = (pair[i * rows : (i + 1) * rows] for i in range(4))
        up = self.hop(one.astype(BF), [(0, 1)])
        down = self.hop(three.astype(BF), [(3, 2)])
        two = (two + up.astype(F4) + down.astype(F4)).astype(BF)
        up = self.hop(two, [(0, 1), (1, 2)])
        down = self.hop(two, [(3, 2), (2, 1)])
        three = three + up.astype(F4)
        one = one + down.astype(F4)
        up = self.hop(three.astype(BF), [(0, 1), (1, 2), (2, 3)])
        down = self.hop(one.astype(BF), [(3, 2), (2, 1), (1, 0)])
        return own + up.astype(F4) + down.astype(F4)

    def chip_groups(self):
        return [list(range(c, self.ns, 2)) for c in range(2)]

    def chips_gather(self, own):
        return lax.all_gather(own, "seq", axis=0, tiled=True, axis_index_groups=self.chip_groups())

    def chips_reduce(self, rows_in):
        return lax.psum_scatter(
            rows_in, "seq", scatter_dimension=0, tiled=True, axis_index_groups=self.chip_groups()
        )

    def bits(self):
        found = []
        bit = self.ns // 2
        while bit:
            found.append(("seq", self.ns, self.s, bit))
            bit //= 2
        bit = self.nz // 2
        while bit:
            found.append(("fsdp", self.nz, self.z, bit))
            bit //= 2
        return found

    def short_gather(self, own):
        held = own[None, :]
        for axis, size, place, bit in reversed(self.bits()):
            other = lax.ppermute(held, axis, [(i, i ^ bit) for i in range(size)])
            high = (place & bit) != 0
            first = jnp.where(high, other, held)
            second = jnp.where(high, held, other)
            held = jnp.concatenate([first, second], 0)
        return held

    def short_reduce(self, held):
        for axis, size, place, bit in self.bits():
            half = held.shape[0] // 2
            high = (place & bit) != 0
            keep = jnp.where(high, held[half:], held[:half])
            send = jnp.where(high, held[:half], held[half:])
            held = keep + lax.ppermute(send, axis, [(i, i ^ bit) for i in range(size)])
        return held[0]


def on_device(
    hidden_in,
    positions,
    norm1_gain,
    norm1_shift,
    w_qkv,
    b_qkv,
    w_out,
    norm2_gain,
    norm2_shift,
    w_gate,
    w_up,
    w_down,
    grad_out,
):
    links = Links()
    ns, nz = links.ns, links.nz
    devices = ns * nz
    chips = ns // 2
    tok_rows = hidden_in.shape[1]
    width = hidden_in.shape[2]
    ff_rows = w_down.shape[0]
    ff_cols = ff_rows * chips
    shard_rows = w_qkv.shape[0]
    seq_places = positions[0]
    length = seq_places.shape[0]
    cols = width // ns
    score_scale = HD ** (-0.5)
    core = links.core

    qkv_blocks = w_qkv.reshape(shard_rows, 3, ns, cols).transpose(2, 0, 1, 3)
    qkv_blocks = qkv_blocks.reshape(ns, shard_rows, 3 * cols)
    qkv_blocks = lax.all_to_all(qkv_blocks, "seq", split_axis=0, concat_axis=0, tiled=True)
    qkv_here = lax.all_gather(qkv_blocks, "fsdp", axis=0, tiled=False)
    qkv_here = qkv_here.transpose(1, 0, 2, 3).reshape(width, 3 * cols)
    out_here = lax.all_gather(w_out, "fsdp", axis=0, tiled=True)

    short = jnp.concatenate([norm1_gain, norm1_shift, norm2_gain, norm2_shift, b_qkv])
    short_all = links.short_gather(short)
    n = shard_rows
    first_gain = short_all[:, :n].reshape(-1)
    first_shift = short_all[:, n : 2 * n].reshape(-1)
    second_gain = short_all[:, 2 * n : 3 * n].reshape(-1)
    second_shift = short_all[:, 3 * n : 4 * n].reshape(-1)
    bias_all = short_all[:, 4 * n :].reshape(3, ns, cols)
    bias_here = lax.dynamic_index_in_dim(bias_all, links.s, 1, keepdims=False).reshape(3 * cols)

    def ff_blocks(weight):
        return weight.reshape(shard_rows, chips, 2, nz, ff_rows).transpose(3, 2, 0, 1, 4)

    gate_up = jnp.stack([ff_blocks(w_gate), ff_blocks(w_up)], 2)
    gate_up = gate_up.reshape(nz, 2, 2, shard_rows, ff_cols)
    gate_up = lax.all_to_all(gate_up, "fsdp", split_axis=0, concat_axis=0, tiled=True)
    ff_keep = jnp.where(core == 0, gate_up[:, 0], gate_up[:, 1])
    ff_send = jnp.where(core == 0, gate_up[:, 1], gate_up[:, 0])
    ff_other = links.swap_core(ff_send)
    ff_first = jnp.where(core == 0, ff_keep, ff_other)
    ff_second = jnp.where(core == 0, ff_other, ff_keep)
    down_here = links.chips_gather(w_down)

    def ff_weight(index):
        rows = jnp.stack([ff_first[:, index], ff_second[:, index]], 0)
        return links.chips_gather(rows.reshape(2 * nz * shard_rows, ff_cols))

    gate_here = ff_weight(0)
    up_here = ff_weight(1)

    inputs = hidden_in.reshape(tok_rows, width).astype(F4)
    first_normed, first_hat, first_inverse = layer_norm(inputs, first_gain, first_shift)
    normed_rows = links.plane_gather(first_normed.astype(BF))
    cotangent_low = grad_out.reshape(tok_rows, width)
    cotangent_rows = links.line_gather(cotangent_low)
    projected = dot(normed_rows, qkv_here) + bias_here.astype(F4)
    projected = links.plane_sorted(projected)
    cosine, sine = angle_tables(seq_places)
    query_heads = rotate(projected[:, :cols], cosine, sine, False).astype(BF).reshape(length, -1, HD)
    all_keys = (
        rotate(projected[:, cols : 2 * cols], cosine, sine, False).astype(BF).reshape(length, -1, HD)
    )
    all_values = projected[:, 2 * cols :].astype(BF).reshape(length, -1, HD)
    heads_out, log_totals = attend(query_heads, all_keys, all_values, seq_places, score_scale)
    mixed = links.plane_unsorted(heads_out)
    half = length // 2
    out_send = dot(mixed[half:], out_here)
    out_keep = dot(mixed[:half], out_here)
    middle = inputs + links.plane_reduce(out_keep, out_send)

    second_normed, second_hat, second_inverse = layer_norm(middle, second_gain, second_shift)
    second_rows = links.line_gather(second_normed.astype(BF))
    d_hidden = dot_nt(cotangent_rows, down_here)
    gate_act = dot(second_rows, gate_here)
    up_act = dot(second_rows, up_here)
    gate_sigmoid = 1.0 / (1.0 + jnp.exp(-gate_act))
    hidden_mid = (gate_act / (1.0 + jnp.exp(-gate_act)) * up_act).astype(BF)
    d_gate = (d_hidden * up_act * gate_sigmoid * (1.0 + gate_act * (1.0 - gate_sigmoid))).astype(BF)
    d_up = (d_hidden * gate_act * gate_sigmoid).astype(BF)
    tokens_half = second_rows.shape[0] // 2

    def second_terms(rows):
        return dot_nt(d_gate[rows], gate_here) + dot_nt(d_up[rows], up_here)

    second_send = second_terms(slice(tokens_half, None))
    second_keep = second_terms(slice(0, tokens_half))
    d_second = links.line_reduce(second_keep, second_send)
    d_from_norm, second_gain_grad, second_shift_grad = norm_backward(
        d_second, second_hat, second_inverse, second_gain
    )
    d_middle = cotangent_low.astype(F4) + d_from_norm
    d_middle_rows = links.plane_gather(d_middle.astype(BF))

    down_share = links.chips_reduce(dot_tn(hidden_mid, cotangent_rows).astype(BF))
    gate_sum = links.chips_reduce(dot_tn(second_rows, d_gate).astype(BF))
    up_sum = links.chips_reduce(dot_tn(second_rows, d_up).astype(BF))
    down_send = dot(hidden_mid[tokens_half:], down_here)
    down_keep = dot(hidden_mid[:tokens_half], down_here)
    layer_out = (middle + links.line_reduce(down_keep, down_send)).astype(BF)

    grad_mixed = dot_nt(d_middle_rows, out_here).astype(BF)
    grad_heads = links.plane_sorted(grad_mixed).reshape(length, -1, HD)
    out_share = lax.psum_scatter(
        dot_tn(mixed, d_middle_rows).astype(BF), "fsdp", scatter_dimension=0, tiled=True
    )
    query_grad, key_grad, value_grad = attend_backward(
        query_heads, all_keys, all_values, grad_heads, log_totals, seq_places, score_scale
    )
    d_projected = jnp.concatenate(
        [
            rotate(query_grad.astype(F4), cosine, sine, True),
            rotate(key_grad.astype(F4), cosine, sine, True),
            value_grad.astype(F4),
        ],
        1,
    ).astype(BF)
    bias_grad = jnp.sum(d_projected.astype(F4), axis=0).reshape(3, 1, cols)
    d_projected = links.plane_unsorted(d_projected)
    qkv_grad = dot_tn(normed_rows, d_projected).astype(BF)
    qkv_grad = qkv_grad.reshape(ns, nz, shard_rows, 3 * cols).transpose(1, 0, 2, 3)
    qkv_sum = lax.psum_scatter(qkv_grad, "fsdp", scatter_dimension=0, tiled=True)
    qkv_sum = qkv_sum.reshape(ns, shard_rows, 3 * cols)
    qkv_sum = lax.all_to_all(qkv_sum, "seq", split_axis=0, concat_axis=0, tiled=True)
    qkv_share = qkv_sum.reshape(ns, shard_rows, 3, cols).transpose(1, 2, 0, 3)
    qkv_share = qkv_share.reshape(shard_rows, 3 * width).astype(F4)
    first_send = dot_nt(d_projected[half:], qkv_here)
    first_keep = dot_nt(d_projected[:half], qkv_here)
    d_first = links.plane_reduce(first_keep, first_send)
    d_from_first, first_gain_grad, first_shift_grad = norm_backward(
        d_first, first_hat, first_inverse, first_gain
    )
    grad_in = (d_middle + d_from_first).astype(BF).reshape(1, tok_rows, width)

    ff_sums = jnp.stack([gate_sum, up_sum], 0).reshape(2, 2, nz, shard_rows, ff_cols)
    sums_keep = jnp.where(core == 0, ff_sums[:, 0], ff_sums[:, 1])
    sums_send = jnp.where(core == 0, ff_sums[:, 1], ff_sums[:, 0])
    sums_other = links.swap_core(sums_send)
    sums_first = jnp.where(core == 0, sums_keep, sums_other)
    sums_second = jnp.where(core == 0, sums_other, sums_keep)
    ff_sums = jnp.stack([sums_first, sums_second], 0).transpose(2, 0, 1, 3, 4)
    ff_sums = lax.all_to_all(ff_sums, "fsdp", split_axis=0, concat_axis=0, tiled=True)

    def ff_share(index):
        blocks = ff_sums[:, :, index].reshape(nz, 2, shard_rows, chips, ff_rows)
        return blocks.transpose(2, 3, 1, 0, 4).reshape(shard_rows, devices * ff_rows).astype(F4)

    placed = lax.dynamic_update_slice(
        jnp.zeros((3, ns, cols), F4), bias_grad, (0, links.s, 0)
    ).reshape(devices, -1)
    short_terms = jnp.concatenate(
        [
            first_gain_grad.reshape(devices, n),
            first_shift_grad.reshape(devices, n),
            second_gain_grad.reshape(devices, n),
            second_shift_grad.reshape(devices, n),
            placed,
        ],
        1,
    )
    short_sums = links.short_reduce(short_terms)
    return (
        layer_out.reshape(1, tok_rows, width),
        grad_in,
        short_sums[:n],
        short_sums[n : 2 * n],
        qkv_share,
        short_sums[4 * n :],
        out_share.astype(F4),
        short_sums[2 * n : 3 * n],
        short_sums[3 * n : 4 * n],
        ff_share(0),
        ff_share(1),
        down_share.astype(F4),
    )


def solution(mesh):
    both = ("seq", "fsdp")
    rows = P("fsdp", "seq", None)
    vector = P(both)
    matrix = P(both, None)
    return jax.shard_map(
        on_device,
        mesh=mesh,
        in_specs=(
            rows,
            P("fsdp", None),
            vector,
            vector,
            matrix,
            vector,
            matrix,
            vector,
            vector,
            matrix,
            matrix,
            matrix,
            rows,
        ),
        out_specs=(
            rows,
            rows,
            vector,
            vector,
            matrix,
            vector,
            matrix,
            vector,
            vector,
            matrix,
            matrix,
            matrix,
        ),
        check_vma=False,
    )
```

```python
import jax
import jax.numpy as jnp
from jax import lax
from jax.experimental import pallas as pl
from jax.experimental.pallas import tpu as pltpu
from jax.sharding import PartitionSpec as P

HD = 64
ROT = 16

EPS = 1e-05
NEG = -1e30

BF = jnp.bfloat16
F4 = jnp.float32


def dot(a, b, out=F4):
    return jnp.dot(a, b, preferred_element_type=F4).astype(out)


def dot_nt(a, b):
    return lax.dot_general(a, b, (((1,), (1,)), ((), ())), preferred_element_type=F4)


def dot_tn(a, b):
    return lax.dot_general(a, b, (((0,), (0,)), ((), ())), preferred_element_type=F4)


def layer_norm(values, gain_row, shift_row):
    row_mean = jnp.mean(values, axis=1, keepdims=True)
    centred = values - row_mean
    inverse = lax.rsqrt(jnp.mean(centred * centred, axis=1, keepdims=True) + EPS)
    normed = centred * inverse
    return (normed * gain_row.astype(F4) + shift_row.astype(F4), normed, inverse)


def norm_backward(grad_rows, normed, inverse, gain_row):
    scaled = grad_rows * gain_row.astype(F4)
    inner_term = (
        scaled
        - jnp.mean(scaled, axis=1, keepdims=True)
        - normed * jnp.mean(scaled * normed, axis=1, keepdims=True)
    )
    return (inner_term * inverse, jnp.sum(grad_rows * normed, axis=0), jnp.sum(grad_rows, axis=0))


def angle_tables(places):
    half_rot = ROT // 2
    frequency = 10000.0 ** (-2.0 * jnp.arange(half_rot, dtype=F4) / ROT)
    angles = places.astype(F4)[:, None] * frequency[None, :]
    return (
        jnp.concatenate([jnp.cos(angles), jnp.cos(angles)], 1),
        jnp.concatenate([jnp.sin(angles), jnp.sin(angles)], 1),
    )


def busy(microseconds):
    return pl.CostEstimate(
        flops=int(microseconds * 1e9), bytes_accessed=0, transcendentals=0
    )


VMEM_BYTES = 56 << 20
BLOCK = 256


def kernel_dot(a, b, contract):
    return lax.dot_general(a, b, (contract, ((), ())), preferred_element_type=F4)


NN = ((1,), (0,))
NT = ((1,), (1,))


def copy_all(pairs, sems):
    copies = [pltpu.make_async_copy(a, b, sems.at[i]) for i, (a, b) in enumerate(pairs)]
    for copy in copies:
        copy.start()
    for copy in copies:
        copy.wait()


def piece_rows(place, pieces, chunk):
    return [
        0 if at is None else pl.multiple_of((place ^ at) * chunk + start, 16)
        for _, at, start in pieces
    ]


def turned(rows, tables, backward):
    plain, ahead, behind = tables
    width = rows.shape[1]
    half = ROT // 2
    moved = pltpu.roll(rows, width - half, 1) * ahead + pltpu.roll(rows, half, 1) * behind
    return rows * plain - moved if backward else rows * plain + moved


def rotary_tables(places, cols):
    half = ROT // 2
    cosine, sine = angle_tables(places)
    rows = places.shape[0]
    rest = jnp.zeros((rows, HD - ROT), F4)
    none = jnp.zeros((rows, half), F4)
    plain = jnp.concatenate([cosine, rest + 1.0], 1)
    ahead = jnp.concatenate([-sine[:, :half], none, rest], 1)
    behind = jnp.concatenate([none, sine[:, half:], rest], 1)
    return [jnp.tile(table, (1, cols // HD)) for table in (plain, ahead, behind)]


def head_lanes(shape, head):
    return lax.broadcasted_iota(jnp.int32, shape, 1) // HD == head


def attend(place, pieces, gain, shift, qkv_line, bias, tables, order, chunk):
    line, plane, shard, three = qkv_line.shape
    cols = three // 3
    width = line * plane * shard
    length = tables[0].shape[0]
    heads = cols // HD
    count = len(pieces)
    block = min(BLOCK, length)
    score_scale = HD ** (-0.5)

    def kernel(place_ref, *refs):
        piece_refs = refs[:count]
        w_ref, gain_ref, shift_ref, bias_ref, plain_ref, ahead_ref, behind_ref = refs[
            count : count + 7
        ]
        n_ref, q_ref, k_ref, v_ref, o_ref, rel_ref, lse_ref, w_held, sems = refs[count + 7 :]
        here = place_ref[0]
        starts = piece_rows(here, pieces, chunk)
        pairs = [
            (ref, n_ref.at[pl.ds(at, ref.shape[0])]) for ref, at in zip(piece_refs, starts)
        ]
        for f in range(line):
            for s in range(plane):
                pairs.append((w_ref.at[f, s], w_held.at[pl.ds((s * line + f) * shard, shard)]))
        copy_all(pairs, sems)

        def project(i, carry):
            rows = pl.ds(pl.multiple_of(i * block, block), block)
            raw = n_ref[rows, :].astype(F4)
            centred = raw - jnp.mean(raw, axis=1, keepdims=True)
            inverse = lax.rsqrt(jnp.mean(centred * centred, axis=1, keepdims=True) + EPS)
            normed = (centred * inverse * gain_ref[...] + shift_ref[...]).astype(BF)
            n_ref[rows, :] = normed
            found = kernel_dot(normed, w_held[...], NN) + bias_ref[...]
            factors = (plain_ref[rows, :], ahead_ref[rows, :], behind_ref[rows, :])
            q_ref[rows, :] = turned(found[:, :cols], factors, False).astype(BF)
            k_ref[rows, :] = turned(found[:, cols : 2 * cols], factors, False).astype(BF)
            v_ref[rows, :] = found[:, 2 * cols :].astype(BF)
            return carry

        lax.fori_loop(0, length // block, project, 0)
        for i in range(length // block):
            rows = slice(i * block, (i + 1) * block)
            seen = (i + 1) * block
            q_rows = q_ref[rows, :]
            k_rows = k_ref[:seen, :]
            v_rows = v_ref[:seen, :]
            allowed = (
                lax.broadcasted_iota(jnp.int32, (block, seen), 1)
                <= lax.broadcasted_iota(jnp.int32, (block, seen), 0) + i * block
            )
            found = jnp.zeros((block, cols), F4)
            totals = jnp.zeros((block, 128), F4)
            for h in range(heads):
                mine = head_lanes((block, cols), h)
                scores = kernel_dot(jnp.where(mine, q_rows, jnp.zeros_like(q_rows)), k_rows, NT)
                scores = jnp.where(allowed, scores * score_scale, NEG)
                peak = jnp.max(scores, axis=1, keepdims=True)
                weights = jnp.exp(scores - peak)
                total = jnp.sum(weights, axis=1, keepdims=True)
                weights = (weights * (1.0 / total)).astype(BF)
                found = jnp.where(mine, kernel_dot(weights, v_rows, NN), found)
                lane = lax.broadcasted_iota(jnp.int32, (block, 128), 1)
                totals = jnp.where(lane == h, peak + jnp.log(total), totals)
            o_ref[rows, :] = found.astype(BF)
            lse_ref[rows, :] = totals
        if order is None:
            rel_ref[...] = o_ref[...]
        else:
            for k, at in enumerate(order):
                start = pl.multiple_of((here ^ at) * chunk, chunk)
                rel_ref[pl.ds(k * chunk, chunk), :] = o_ref[pl.ds(start, chunk), :]

    anywhere = pl.BlockSpec(memory_space=pl.ANY)
    whole = pl.BlockSpec(memory_space=pltpu.VMEM)
    tall = jax.ShapeDtypeStruct((length, cols), BF)
    return pl.pallas_call(
        kernel,
        out_shape=[
            jax.ShapeDtypeStruct((length, width), BF),
            tall,
            tall,
            tall,
            tall,
            tall,
            jax.ShapeDtypeStruct((length, 128), F4),
        ],
        in_specs=[pl.BlockSpec(memory_space=pltpu.SMEM)] + [anywhere] * (count + 1) + [whole] * 6,
        out_specs=[whole] * 7,
        scratch_shapes=[
            pltpu.VMEM((width, three), BF),
            pltpu.SemaphoreType.DMA((count + line * plane,)),
        ],
        compiler_params=pltpu.CompilerParams(vmem_limit_bytes=VMEM_BYTES),
        cost_estimate=busy(17),
        name="attend",
    )(place, *[piece for piece, _, _ in pieces], qkv_line, gain, shift, bias, *tables)


def attend_back(place, pieces, out_here, q, k, v, lse, tables, order, chunk):
    length, cols = q.shape
    width = out_here.shape[1]
    heads = cols // HD
    count = len(pieces)
    block = min(BLOCK, length)
    score_scale = HD ** (-0.5)

    def kernel(place_ref, *refs):
        piece_refs = refs[:count]
        out_ref, q_ref, k_ref, v_ref, lse_ref, plain_ref, ahead_ref, behind_ref = refs[
            count : count + 8
        ]
        d_ref, all_ref, rel_ref, sum_ref, do_ref, delta_ref, dq_ref, dk_ref, sems = refs[count + 8 :]
        here = place_ref[0]
        starts = piece_rows(here, pieces, chunk)
        copy_all(
            [(ref, d_ref.at[pl.ds(at, ref.shape[0])]) for ref, at in zip(piece_refs, starts)], sems
        )

        def project(i, carry):
            rows = pl.ds(pl.multiple_of(i * block, block), block)
            do_ref[rows, :] = kernel_dot(d_ref[rows, :], out_ref[...], NT).astype(BF)
            return carry

        lax.fori_loop(0, length // block, project, 0)
        for i in range(length // block):
            rows = slice(i * block, (i + 1) * block)
            seen = (i + 1) * block
            q_rows, do_rows = q_ref[rows, :], do_ref[rows, :]
            k_rows, v_rows = k_ref[:seen, :], v_ref[:seen, :]
            allowed = (
                lax.broadcasted_iota(jnp.int32, (block, seen), 1)
                <= lax.broadcasted_iota(jnp.int32, (block, seen), 0) + i * block
            )
            found = jnp.zeros((block, cols), F4)
            deltas = jnp.zeros((block, 128), F4)
            for h in range(heads):
                mine = head_lanes((block, cols), h)
                none = jnp.zeros_like(q_rows)
                scores = kernel_dot(jnp.where(mine, q_rows, none), k_rows, NT) * score_scale
                probs = jnp.where(allowed, jnp.exp(scores - lse_ref[rows, h : h + 1]), 0.0)
                d_probs = kernel_dot(jnp.where(mine, do_rows, none), v_rows, NT)
                delta = jnp.sum(probs * d_probs, axis=1, keepdims=True)
                d_scores = (probs * (d_probs - delta)).astype(BF)
                found = jnp.where(mine, kernel_dot(d_scores, k_rows, NN), found)
                lane = lax.broadcasted_iota(jnp.int32, (block, 128), 1)
                deltas = jnp.where(lane == h, delta, deltas)
            dq_ref[rows, :] = (found * score_scale).astype(BF)
            delta_ref[rows, :] = deltas
        lse_rows = jnp.transpose(lse_ref[...])
        delta_rows = jnp.transpose(delta_ref[...])
        for j in range(length // block):
            rows = slice(j * block, (j + 1) * block)
            left = length - j * block
            k_rows, v_rows = k_ref[rows, :], v_ref[rows, :]
            q_rows, do_rows = q_ref[j * block :, :], do_ref[j * block :, :]
            allowed = lax.broadcasted_iota(jnp.int32, (block, left), 0) <= lax.broadcasted_iota(
                jnp.int32, (block, left), 1
            )
            keys = jnp.zeros((block, cols), F4)
            values = jnp.zeros((block, cols), F4)
            for h in range(heads):
                mine = head_lanes((block, cols), h)
                none = jnp.zeros_like(k_rows)
                scores = kernel_dot(jnp.where(mine, k_rows, none), q_rows, NT) * score_scale
                lse_row = lse_rows[h : h + 1, j * block :]
                probs = jnp.where(allowed, jnp.exp(scores - lse_row), 0.0)
                d_probs = kernel_dot(jnp.where(mine, v_rows, none), do_rows, NT)
                d_scores = (probs * (d_probs - delta_rows[h : h + 1, j * block :])).astype(BF)
                keys = jnp.where(mine, kernel_dot(d_scores, q_rows, NN), keys)
                values = jnp.where(mine, kernel_dot(probs.astype(BF), do_rows, NN), values)
            dk_ref[rows, :] = (keys * score_scale).astype(BF)
            all_ref[rows, 2 * cols :] = values.astype(BF)

        sum_ref[...] = jnp.zeros_like(sum_ref)

        def finish(i, carry):
            rows = pl.ds(pl.multiple_of(i * block, block), block)
            factors = (plain_ref[rows, :], ahead_ref[rows, :], behind_ref[rows, :])
            all_ref[rows, :cols] = turned(dq_ref[rows, :].astype(F4), factors, True).astype(BF)
            all_ref[rows, cols : 2 * cols] = turned(
                dk_ref[rows, :].astype(F4), factors, True
            ).astype(BF)
            sum_ref[...] += jnp.sum(all_ref[rows, :].astype(F4), axis=0, keepdims=True)
            return carry

        lax.fori_loop(0, length // block, finish, 0)
        if order is None:
            rel_ref[...] = all_ref[...]
        else:
            for n, at in enumerate(order):
                start = pl.multiple_of((here ^ at) * chunk, chunk)
                rel_ref[pl.ds(n * chunk, chunk), :] = all_ref[pl.ds(start, chunk), :]

    anywhere = pl.BlockSpec(memory_space=pl.ANY)
    whole = pl.BlockSpec(memory_space=pltpu.VMEM)
    wide = jax.ShapeDtypeStruct((length, 3 * cols), BF)
    return pl.pallas_call(
        kernel,
        out_shape=[
            jax.ShapeDtypeStruct((length, width), BF),
            wide,
            wide,
            jax.ShapeDtypeStruct((1, 3 * cols), F4),
        ],
        in_specs=[pl.BlockSpec(memory_space=pltpu.SMEM)] + [anywhere] * count + [whole] * 8,
        out_specs=[whole] * 4,
        scratch_shapes=[
            pltpu.VMEM((length, cols), BF),
            pltpu.VMEM((length, 128), F4),
            pltpu.VMEM((length, cols), BF),
            pltpu.VMEM((length, cols), BF),
            pltpu.SemaphoreType.DMA((count,)),
        ],
        compiler_params=pltpu.CompilerParams(vmem_limit_bytes=VMEM_BYTES),
        cost_estimate=busy(26),
        name="attend_back",
    )(place, *[piece for piece, _, _ in pieces], out_here, q, k, v, lse, *tables)


def outer_rows(left, pieces):
    count = len(pieces)
    starts, length = [], 0
    for piece in pieces:
        starts.append(length)
        length += piece.shape[0]
    cols, width = left.shape[1], pieces[0].shape[1]

    def kernel(left_ref, *refs):
        held, sems = refs[count + 1 :]
        copy_all(
            [(ref, held.at[pl.ds(at, ref.shape[0])]) for ref, at in zip(refs[:count], starts)], sems
        )
        refs[count][...] = kernel_dot(left_ref[...], held[...], ((0,), (0,))).astype(BF)

    anywhere = pl.BlockSpec(memory_space=pl.ANY)
    whole = pl.BlockSpec(memory_space=pltpu.VMEM)
    return pl.pallas_call(
        kernel,
        out_shape=jax.ShapeDtypeStruct((cols, width), BF),
        in_specs=[whole] + [anywhere] * count,
        out_specs=whole,
        scratch_shapes=[pltpu.VMEM((length, width), BF), pltpu.SemaphoreType.DMA((count,))],
        compiler_params=pltpu.CompilerParams(vmem_limit_bytes=VMEM_BYTES),
        cost_estimate=busy(4),
        name="outer_rows",
    )(left, *pieces)


def feed(pieces, grads, ff_line):
    line, plane, shard, both = ff_line.shape
    cols = both // 2
    width = line * plane * shard
    count = len(pieces)
    starts, length = [], 0
    for piece in pieces:
        starts.append(length)
        length += piece.shape[0]
    block = min(512, length)
    copies = 2 * count + line * plane

    def kernel(*refs):
        piece_refs, grad_refs = refs[:count], refs[count : 2 * count]
        ff_ref = refs[2 * count]
        n_ref, g_ref, a_ref, both_ref, w_held, sems = refs[2 * count + 1 :]
        pairs = []
        for f in range(line):
            for s in range(plane):
                pairs.append((ff_ref.at[f, s], w_held.at[pl.ds((s * line + f) * shard, shard)]))
        for held, found in ((n_ref, piece_refs), (g_ref, grad_refs)):
            for ref, at in zip(found, starts):
                pairs.append((ref, held.at[pl.ds(at, ref.shape[0])]))
        copy_all(pairs, sems)

        def step(i, carry):
            rows = pl.ds(pl.multiple_of(i * block, block), block)
            gate_up = kernel_dot(n_ref[rows, :], w_held[...], NN)
            both_ref[rows, :] = gate_up
            gate, up = gate_up[:, :cols], gate_up[:, cols:]
            a_ref[rows, :] = (gate / (1.0 + jnp.exp(-gate)) * up).astype(BF)
            return carry

        lax.fori_loop(0, length // block, step, 0)

    anywhere = pl.BlockSpec(memory_space=pl.ANY)
    whole = pl.BlockSpec(memory_space=pltpu.VMEM)
    return pl.pallas_call(
        kernel,
        out_shape=[
            jax.ShapeDtypeStruct((length, width), BF),
            jax.ShapeDtypeStruct((length, width), BF),
            jax.ShapeDtypeStruct((length, cols), BF),
            jax.ShapeDtypeStruct((length, both), F4),
        ],
        in_specs=[anywhere] * (2 * count + 1),
        out_specs=[whole] * 4,
        scratch_shapes=[pltpu.VMEM((width, both), BF), pltpu.SemaphoreType.DMA((copies,))],
        compiler_params=pltpu.CompilerParams(vmem_limit_bytes=VMEM_BYTES),
        cost_estimate=busy(17),
        name="feed",
    )(*pieces, *grads, ff_line)


def feed_back(grad_rows, gate_up, ff_line, down_here):
    line, plane, shard, both = ff_line.shape
    cols = both // 2
    length, width = grad_rows.shape
    half = length // 2
    block = min(512, half)

    def kernel(g_ref, both_ref, ff_ref, down_ref, d_ref, send_ref, keep_ref, w_held, sems):
        pairs = []
        for f in range(line):
            for s in range(plane):
                pairs.append((ff_ref.at[f, s], w_held.at[pl.ds((s * line + f) * shard, shard)]))
        copies = [pltpu.make_async_copy(a, b, sems.at[i]) for i, (a, b) in enumerate(pairs)]
        for copy in copies:
            copy.start()

        def step(i, carry):
            rows = pl.ds(pl.multiple_of(i * block, block), block)
            d_hidden = kernel_dot(g_ref[rows, :], down_ref[...], NT)
            gate, up = both_ref[rows, :cols], both_ref[rows, cols:]
            sigmoid = 1.0 / (1.0 + jnp.exp(-gate))
            d_gate = d_hidden * up * sigmoid * (1.0 + gate * (1.0 - sigmoid))
            d_ref[rows, :] = jnp.concatenate([d_gate, d_hidden * gate * sigmoid], 1).astype(BF)
            return carry

        lax.fori_loop(0, length // block, step, 0)
        for copy in copies:
            copy.wait()

        def back(i, carry):
            rows = pl.ds(pl.multiple_of(i * block, block), block)
            there = pl.ds(pl.multiple_of(half + i * block, block), block)
            send_ref[rows, :] = kernel_dot(d_ref[there, :], w_held[...], NT).astype(BF)
            keep_ref[rows, :] = kernel_dot(d_ref[rows, :], w_held[...], NT)
            return carry

        lax.fori_loop(0, half // block, back, 0)

    anywhere = pl.BlockSpec(memory_space=pl.ANY)
    whole = pl.BlockSpec(memory_space=pltpu.VMEM)
    return pl.pallas_call(
        kernel,
        out_shape=[
            jax.ShapeDtypeStruct((length, both), BF),
            jax.ShapeDtypeStruct((half, width), BF),
            jax.ShapeDtypeStruct((half, width), F4),
        ],
        in_specs=[whole, whole, anywhere, whole],
        out_specs=[whole] * 3,
        scratch_shapes=[
            pltpu.VMEM((width, both), BF),
            pltpu.SemaphoreType.DMA((line * plane,)),
        ],
        compiler_params=pltpu.CompilerParams(vmem_limit_bytes=VMEM_BYTES),
        cost_estimate=busy(17),
        name="feed_back",
    )(grad_rows, gate_up, ff_line, down_here)


def nothing(*refs):
    pass


def turn(values, *earlier):
    anywhere = pl.BlockSpec(memory_space=pl.ANY)
    return pl.pallas_call(
        nothing,
        out_shape=[jax.ShapeDtypeStruct(v.shape, v.dtype) for v in values],
        in_specs=[anywhere] * (len(values) + len(earlier)),
        out_specs=[anywhere] * len(values),
        input_output_aliases={i: i for i in range(len(values))},
        cost_estimate=pl.CostEstimate(flops=0, bytes_accessed=0, transcendentals=0),
        name="in_turn",
    )(*values, *earlier)


def after(values, *earlier):
    return turn([values], *earlier)[0]


def pair_columns(gate, up, lists):
    rows, width = gate.shape
    part = width // sum(len(blocks) for blocks in lists)

    def kernel(gate_ref, up_ref, blocks_ref):
        whole = [gate_ref[...].astype(F4), up_ref[...].astype(F4)]
        for i, blocks in enumerate(lists):
            columns = [w[:, at * part : (at + 1) * part] for w in whole for at in blocks]
            blocks_ref[i] = jnp.concatenate(columns, 1).astype(BF)

    held = 2 * part * len(lists[0])
    return pl.pallas_call(
        kernel,
        out_shape=jax.ShapeDtypeStruct((len(lists), rows, held), BF),
        compiler_params=pltpu.CompilerParams(vmem_limit_bytes=32 << 20),
        name="pair_columns",
    )(gate, up)


def part_columns(blocks, lists):
    parts, rows, held = blocks.shape
    count = len(lists[0])
    part = held // (2 * count)
    width = parts * count * part
    place = {at: (i, j) for i, each in enumerate(lists) for j, at in enumerate(each)}

    def kernel(blocks_ref, first_ref, second_ref):
        whole = [blocks_ref[i].astype(F4) for i in range(parts)]
        for k, ref in enumerate((first_ref, second_ref)):
            columns = []
            for at in range(parts * count):
                i, j = place[at]
                start = (k * count + j) * part
                columns.append(whole[i][:, start : start + part])
            ref[...] = jnp.concatenate(columns, 1)

    return pl.pallas_call(
        kernel,
        out_shape=[jax.ShapeDtypeStruct((rows, width), F4)] * 2,
        compiler_params=pltpu.CompilerParams(vmem_limit_bytes=32 << 20),
        name="part_columns",
    )(blocks)


class Links:
    def __init__(self):
        self.ns = lax.axis_size("seq")
        self.nz = lax.axis_size("fsdp")
        self.s = lax.axis_index("seq")
        self.z = lax.axis_index("fsdp")
        self.core = self.s % 2
        self.fast_plane = self.ns == 8
        self.order = [0, 2, 4, 6, 1, 3, 5, 7]

    def flip(self, values, bit):
        return lax.ppermute(values, "seq", [(i, i ^ bit) for i in range(self.ns)])

    def swap_core(self, values):
        return self.flip(values, 1)

    def hop(self, values, pairs):
        return lax.ppermute(values, "fsdp", pairs)

    def along_x(self, values):
        return self.flip(values, 2)

    def along_y(self, values):
        return self.flip(values, 4)

    def square_gather(self, own, one, two, codes):
        cut = own.shape[0] // 32 * 16
        first = one(own)
        second = two(own)
        return [
            (own, 0, 0),
            (first, codes[0], 0),
            (second, codes[1], 0),
            (two(first[:cut]), codes[0] | codes[1], 0),
            (one(second[cut:]), codes[0] | codes[1], cut),
        ]

    def with_core(self, found):
        return found + [(self.swap_core(part), at | 1, start) for part, at, start in found]

    def square_reduce(self, own, first, second, far, one, two):
        return self.square_reduce_end(
            self.square_reduce_start(own, first, second, far, one, two), one, two
        )

    def square_reduce_start(self, own, first, second, far, one, two):
        cut = far.shape[0] // 32 * 16
        far = far.astype(BF)
        via_one = one(far[:cut])
        via_two = two(far[cut:])
        second = jnp.concatenate([second[:cut] + via_one.astype(F4), second[cut:]], 0).astype(BF)
        first = jnp.concatenate([first[:cut], first[cut:] + via_two.astype(F4)], 0).astype(BF)
        return [own, first, second]

    def square_reduce_end(self, parts, one, two):
        own, first, second = parts
        return own + one(first).astype(F4) + two(second).astype(F4)

    def core_sum(self, keep, send, *earlier):
        other = self.swap_core(send.astype(BF))
        return keep + (after(other, *earlier) if earlier else other).astype(F4)

    def plane_gather(self, own):
        if not self.fast_plane:
            return [(lax.all_gather(own, "seq", axis=0, tiled=True), None, 0)]
        return self.with_core(self.square_gather(own, self.along_x, self.along_y, (2, 4)))

    def plane_reduce(self, keep, send):
        if not self.fast_plane:
            terms = jnp.concatenate([keep, send], 0).astype(BF)
            return lax.psum_scatter(terms, "seq", scatter_dimension=0, tiled=True).astype(F4)
        pair = self.core_sum(keep, send)
        rows = pair.shape[0] // 4
        terms = [pair[i * rows : (i + 1) * rows] for i in range(4)]
        return self.square_reduce(*terms, self.along_x, self.along_y)

    def line_gather(self, own):
        return lax.all_gather(own, "fsdp", axis=0, tiled=True)

    def line_reduce(self, terms):
        return lax.psum_scatter(terms, "fsdp", scatter_dimension=0, tiled=True)

    def swap_blocks(self, blocks):
        return lax.all_to_all(blocks, "seq", split_axis=0, concat_axis=0, tiled=True)

    def rows_sorted(self, blocks):
        return blocks.transpose(1, 0, 2, 3).reshape(-1, blocks.shape[3])

    def rows_by_line(self, rows_in, shard_rows):
        shape = (self.ns, self.nz, shard_rows, rows_in.shape[1])
        return rows_in.reshape(shape).transpose(1, 0, 2, 3)

    def ff_lists(self):
        return [[s * self.nz + f for f in range(self.nz)] for s in range(self.ns)]

    def short_gather_line(self, own):
        held = own[None, :]
        for k in range(1, self.nz):
            other = lax.ppermute(own, "fsdp", [(i, i ^ k) for i in range(self.nz)])
            held = jnp.concatenate([held, other[None, :]], 0)
        bit = 1
        while bit < self.nz:
            pairs = held.reshape(-1, 2, bit, own.shape[0])
            held = jnp.where((self.z & bit) != 0, pairs[:, ::-1], pairs).reshape(held.shape)
            bit *= 2
        return held

    def short_gather_plane(self, held):
        bit = 1
        while bit < self.ns:
            other = self.flip(held, bit)
            high = (self.s & bit) != 0
            first = jnp.where(high, other, held)
            second = jnp.where(high, held, other)
            held = jnp.concatenate([first, second], 0)
            bit *= 2
        return held

    def short_reduce(self, held):
        bit = self.ns // 2
        while bit:
            half = held.shape[0] // 2
            high = (self.s & bit) != 0
            keep = jnp.where(high, held[half:], held[:half])
            send = jnp.where(high, held[:half], held[half:])
            held = keep + self.flip(send, bit)
            bit //= 2
        total = lax.dynamic_index_in_dim(held, self.z, 0, keepdims=False)
        for k in range(1, self.nz):
            send = lax.dynamic_index_in_dim(held, self.z ^ k, 0, keepdims=False)
            total = total + lax.ppermute(send, "fsdp", [(i, i ^ k) for i in range(self.nz)])
        return total


def on_device(
    hidden_in,
    positions,
    norm1_gain,
    norm1_shift,
    w_qkv,
    b_qkv,
    w_out,
    norm2_gain,
    norm2_shift,
    w_gate,
    w_up,
    w_down,
    grad_out,
):
    links = Links()
    ns, nz = links.ns, links.nz
    devices = ns * nz
    tok_rows = hidden_in.shape[1]
    width = hidden_in.shape[2]
    shard_rows = w_qkv.shape[0]
    seq_places = positions[0]
    length = seq_places.shape[0]
    cols = width // ns
    score_scale = HD ** (-0.5)

    lists = links.ff_lists()
    out_here = links.line_gather(w_out)
    short = jnp.concatenate([norm1_gain, norm1_shift, norm2_gain, norm2_shift, b_qkv])
    short_line = links.short_gather_line(short)
    qkv_blocks = w_qkv.reshape(shard_rows, 3, ns, cols).transpose(2, 0, 1, 3)
    qkv_blocks = links.swap_blocks(qkv_blocks.reshape(ns, shard_rows, 3 * cols))
    qkv_blocks, short_line = turn([qkv_blocks, short_line], out_here)
    qkv_line = links.line_gather(qkv_blocks[None])
    ff_blocks = links.swap_blocks(pair_columns(w_gate, w_up, lists))

    short_all = links.short_gather_plane(short_line)
    short_all, w_down = turn([short_all, w_down])
    n = shard_rows
    first_gain = short_all[:, :n].reshape(-1)
    first_shift = short_all[:, n : 2 * n].reshape(-1)
    second_gain = short_all[:, 2 * n : 3 * n].reshape(-1)
    second_shift = short_all[:, 3 * n : 4 * n].reshape(-1)
    bias_all = short_all[:, 4 * n :].reshape(3, ns, cols)
    bias_here = lax.dynamic_index_in_dim(bias_all, links.s, 1, keepdims=False).reshape(3 * cols)

    place = jnp.stack([links.s, links.z]).astype(jnp.int32)
    order = links.order if links.fast_plane else None
    inputs = hidden_in.reshape(tok_rows, width).astype(F4)
    _, first_hat, first_inverse = layer_norm(inputs, first_gain, first_shift)
    first_pieces = links.plane_gather(hidden_in.reshape(tok_rows, width))
    cotangent_low = grad_out.reshape(tok_rows, width)
    tables = rotary_tables(seq_places, cols)
    half = length // 2

    def let(values, *earlier):
        flat = turn([v for group in values for v in group], *earlier)
        found = []
        for group in values:
            found.append(list(flat[: len(group)]))
            flat = flat[len(group) :]
        return found

    def arrays(pieces):
        return [piece for piece, _, _ in pieces]

    def renewed(pieces, values):
        return [(value, at, start) for value, (_, at, start) in zip(values, pieces)]

    vectors = [v.astype(F4)[None] for v in (first_gain, first_shift, bias_here)]
    found, vectors, (ff_blocks, cotangent_low) = let(
        [arrays(first_pieces), vectors, [ff_blocks, cotangent_low]]
    )
    found, vectors, (ff_blocks, w_down, cotangent_low) = let(
        [found, vectors, [ff_blocks, w_down, cotangent_low]], qkv_line
    )
    first_pieces = renewed(first_pieces, found)
    ff_line = links.line_gather(ff_blocks[None])
    down_here = links.line_gather(after(w_down, ff_line))
    cotangent_pieces = arrays(links.plane_gather(cotangent_low))
    normed_rows, queries, keys, values, mixed, mixed_rel, log_totals = attend(
        place,
        first_pieces,
        vectors[0],
        vectors[1],
        qkv_line,
        vectors[2],
        tables,
        order,
        tok_rows,
    )
    out_send = dot(mixed_rel[half:], out_here, BF)
    out_keep = dot(mixed_rel[:half], out_here)
    middle = inputs + links.plane_reduce(out_keep, out_send)

    second_normed, second_hat, second_inverse = layer_norm(middle, second_gain, second_shift)
    second_low = second_normed.astype(BF)
    second_pieces = arrays(links.plane_gather(second_low))
    second_rows, cotangent_rows, hidden_mid, gate_up = feed(
        second_pieces, cotangent_pieces, ff_line
    )
    down_grad = dot_tn(hidden_mid, cotangent_rows).astype(BF)
    down_sum = links.line_reduce(down_grad)
    grad_rows, gate_up = turn([cotangent_rows, gate_up], down_grad)
    d_ff, second_send, second_keep = feed_back(grad_rows, gate_up, ff_line, down_here)
    ff_grad = links.rows_by_line(dot_tn(second_rows, d_ff).astype(BF), shard_rows)
    ff_sum = links.line_reduce(after(ff_grad, down_sum)).reshape(ns, shard_rows, -1)
    second_send, second_keep = turn([second_send, second_keep], ff_grad)
    d_second = links.plane_reduce(second_keep, second_send)
    d_second = after(d_second, down_sum)
    d_from_norm, second_gain_grad, second_shift_grad = norm_backward(
        d_second, second_hat, second_inverse, second_gain
    )
    d_middle = cotangent_low.astype(F4) + d_from_norm
    d_middle_pieces = links.plane_gather(d_middle.astype(BF))
    out_grad = outer_rows(mixed_rel, arrays(d_middle_pieces))
    d_middle_rows, d_projected, d_projected_rel, bias_grad = attend_back(
        place,
        d_middle_pieces,
        out_here,
        queries,
        keys,
        values,
        log_totals,
        tables,
        order,
        tok_rows,
    )
    qkv_here = links.rows_sorted(qkv_line)
    first_send = dot_nt(d_projected_rel[half:], qkv_here).astype(BF)
    d_projected = after(d_projected, first_send)
    qkv_grad = links.rows_by_line(dot_tn(normed_rows, d_projected).astype(BF), shard_rows)
    qkv_sum = links.line_reduce(after(qkv_grad, ff_sum))
    out_share = links.line_reduce(after(out_grad, qkv_sum))
    qkv_sum = qkv_sum.reshape(ns, shard_rows, -1)
    bias_grad = bias_grad.reshape(3, 1, cols)

    hidden_later = after(hidden_mid, d_middle_rows)
    layer_send = dot(hidden_later[half:], down_here, BF)
    layer_keep = dot(hidden_later[:half], down_here)
    layer_out = (middle + links.plane_reduce(layer_keep, layer_send)).astype(BF)

    first_keep = dot_nt(d_projected_rel[:half], qkv_here)
    d_first = links.plane_reduce(first_keep, first_send)
    d_from_first, first_gain_grad, first_shift_grad = norm_backward(
        d_first, first_hat, first_inverse, first_gain
    )
    grad_in = (d_middle + d_from_first).astype(BF).reshape(1, tok_rows, width)

    placed = lax.dynamic_update_slice(
        jnp.zeros((3, ns, cols), F4), bias_grad, (0, links.s, 0)
    ).reshape(devices, -1)
    short_terms = jnp.concatenate(
        [
            first_gain_grad.reshape(devices, n),
            first_shift_grad.reshape(devices, n),
            second_gain_grad.reshape(devices, n),
            second_shift_grad.reshape(devices, n),
            placed,
        ],
        1,
    )
    short_sums = links.short_reduce(short_terms)

    gate_share, up_share = part_columns(links.swap_blocks(ff_sum), lists)
    qkv_share = links.swap_blocks(qkv_sum).reshape(ns, shard_rows, 3, cols).transpose(1, 2, 0, 3)
    qkv_share = qkv_share.reshape(shard_rows, 3 * width).astype(F4)
    return (
        layer_out.reshape(1, tok_rows, width),
        grad_in,
        short_sums[:n],
        short_sums[n : 2 * n],
        qkv_share,
        short_sums[4 * n :],
        out_share.astype(F4),
        short_sums[2 * n : 3 * n],
        short_sums[3 * n : 4 * n],
        gate_share,
        up_share,
        down_sum.astype(F4),
    )


def solution(mesh):
    both = ("seq", "fsdp")
    rows = P("fsdp", "seq", None)
    vector = P(both)
    matrix = P(both, None)
    return jax.shard_map(
        on_device,
        mesh=mesh,
        in_specs=(
            rows,
            P("fsdp", None),
            vector,
            vector,
            matrix,
            vector,
            matrix,
            vector,
            vector,
            matrix,
            matrix,
            matrix,
            rows,
        ),
        out_specs=(
            rows,
            rows,
            vector,
            vector,
            matrix,
            vector,
            matrix,
            vector,
            vector,
            matrix,
            matrix,
            matrix,
        ),
        check_vma=False,
    )
```

```python
import jax
import jax.numpy as jnp
from jax import lax
from jax.experimental import pallas as pl
from jax.experimental.pallas import tpu as pltpu
from jax.sharding import PartitionSpec as P

HD = 64
ROT = 16

EPS = 1e-05
NEG = -1e30

BF = jnp.bfloat16
F4 = jnp.float32


def dot(a, b, out=F4):
    return jnp.dot(a, b, preferred_element_type=F4).astype(out)


def dot_nt(a, b):
    return lax.dot_general(a, b, (((1,), (1,)), ((), ())), preferred_element_type=F4)


def dot_tn(a, b):
    return lax.dot_general(a, b, (((0,), (0,)), ((), ())), preferred_element_type=F4)


def layer_norm(values, gain_row, shift_row):
    row_mean = jnp.mean(values, axis=1, keepdims=True)
    centred = values - row_mean
    inverse = lax.rsqrt(jnp.mean(centred * centred, axis=1, keepdims=True) + EPS)
    normed = centred * inverse
    return (normed * gain_row.astype(F4) + shift_row.astype(F4), normed, inverse)


def norm_backward(grad_rows, normed, inverse, gain_row):
    scaled = grad_rows * gain_row.astype(F4)
    inner_term = (
        scaled
        - jnp.mean(scaled, axis=1, keepdims=True)
        - normed * jnp.mean(scaled * normed, axis=1, keepdims=True)
    )
    return (inner_term * inverse, jnp.sum(grad_rows * normed, axis=0), jnp.sum(grad_rows, axis=0))


def angle_tables(places):
    half_rot = ROT // 2
    frequency = 10000.0 ** (-2.0 * jnp.arange(half_rot, dtype=F4) / ROT)
    angles = places.astype(F4)[:, None] * frequency[None, :]
    return (
        jnp.concatenate([jnp.cos(angles), jnp.cos(angles)], 1),
        jnp.concatenate([jnp.sin(angles), jnp.sin(angles)], 1),
    )


def busy(microseconds):
    return pl.CostEstimate(
        flops=int(microseconds * 1e9), bytes_accessed=0, transcendentals=0
    )


VMEM_BYTES = 56 << 20
BLOCK = 256


def kernel_dot(a, b, contract):
    return lax.dot_general(a, b, (contract, ((), ())), preferred_element_type=F4)


NN = ((1,), (0,))
NT = ((1,), (1,))


def copy_all(pairs, sems):
    copies = [pltpu.make_async_copy(a, b, sems.at[i]) for i, (a, b) in enumerate(pairs)]
    for copy in copies:
        copy.start()
    for copy in copies:
        copy.wait()


def piece_rows(place, pieces, chunk):
    return [
        0 if at is None else pl.multiple_of((place ^ at) * chunk + start, 16)
        for _, at, start in pieces
    ]


def turned(rows, tables, backward):
    plain, ahead, behind = tables
    width = rows.shape[1]
    half = ROT // 2
    moved = pltpu.roll(rows, width - half, 1) * ahead + pltpu.roll(rows, half, 1) * behind
    return rows * plain - moved if backward else rows * plain + moved


def rotary_tables(places, cols):
    half = ROT // 2
    cosine, sine = angle_tables(places)
    rows = places.shape[0]
    rest = jnp.zeros((rows, HD - ROT), F4)
    none = jnp.zeros((rows, half), F4)
    plain = jnp.concatenate([cosine, rest + 1.0], 1)
    ahead = jnp.concatenate([-sine[:, :half], none, rest], 1)
    behind = jnp.concatenate([none, sine[:, half:], rest], 1)
    return [jnp.tile(table, (1, cols // HD)) for table in (plain, ahead, behind)]


def head_lanes(shape, head):
    return lax.broadcasted_iota(jnp.int32, shape, 1) // HD == head


def attend(place, pieces, gain, shift, qkv_line, bias, tables, order, chunk):
    line, plane, shard, three = qkv_line.shape
    cols = three // 3
    width = line * plane * shard
    length = tables[0].shape[0]
    heads = cols // HD
    count = len(pieces)
    block = min(BLOCK, length)
    score_scale = HD ** (-0.5)

    def kernel(place_ref, *refs):
        piece_refs = refs[:count]
        w_ref, gain_ref, shift_ref, bias_ref, plain_ref, ahead_ref, behind_ref = refs[
            count : count + 7
        ]
        n_ref, q_ref, k_ref, v_ref, o_ref, rel_ref, lse_ref, w_held, sems = refs[count + 7 :]
        here = place_ref[0]
        starts = piece_rows(here, pieces, chunk)
        pairs = [
            (ref, n_ref.at[pl.ds(at, ref.shape[0])]) for ref, at in zip(piece_refs, starts)
        ]
        for f in range(line):
            for s in range(plane):
                pairs.append((w_ref.at[f, s], w_held.at[pl.ds((s * line + f) * shard, shard)]))
        copy_all(pairs, sems)

        def project(i, carry):
            rows = pl.ds(pl.multiple_of(i * block, block), block)
            raw = n_ref[rows, :].astype(F4)
            centred = raw - jnp.mean(raw, axis=1, keepdims=True)
            inverse = lax.rsqrt(jnp.mean(centred * centred, axis=1, keepdims=True) + EPS)
            normed = (centred * inverse * gain_ref[...] + shift_ref[...]).astype(BF)
            n_ref[rows, :] = normed
            found = kernel_dot(normed, w_held[...], NN) + bias_ref[...]
            factors = (plain_ref[rows, :], ahead_ref[rows, :], behind_ref[rows, :])
            q_ref[rows, :] = turned(found[:, :cols], factors, False).astype(BF)
            k_ref[rows, :] = turned(found[:, cols : 2 * cols], factors, False).astype(BF)
            v_ref[rows, :] = found[:, 2 * cols :].astype(BF)
            return carry

        lax.fori_loop(0, length // block, project, 0)
        for i in range(length // block):
            rows = slice(i * block, (i + 1) * block)
            seen = (i + 1) * block
            q_rows = q_ref[rows, :]
            k_rows = k_ref[:seen, :]
            v_rows = v_ref[:seen, :]
            allowed = (
                lax.broadcasted_iota(jnp.int32, (block, seen), 1)
                <= lax.broadcasted_iota(jnp.int32, (block, seen), 0) + i * block
            )
            found = jnp.zeros((block, cols), F4)
            totals = jnp.zeros((block, 128), F4)
            for h in range(heads):
                mine = head_lanes((block, cols), h)
                scores = kernel_dot(jnp.where(mine, q_rows, jnp.zeros_like(q_rows)), k_rows, NT)
                scores = jnp.where(allowed, scores * score_scale, NEG)
                peak = jnp.max(scores, axis=1, keepdims=True)
                weights = jnp.exp(scores - peak)
                total = jnp.sum(weights, axis=1, keepdims=True)
                weights = (weights * (1.0 / total)).astype(BF)
                found = jnp.where(mine, kernel_dot(weights, v_rows, NN), found)
                lane = lax.broadcasted_iota(jnp.int32, (block, 128), 1)
                totals = jnp.where(lane == h, peak + jnp.log(total), totals)
            o_ref[rows, :] = found.astype(BF)
            lse_ref[rows, :] = totals
        if order is None:
            rel_ref[...] = o_ref[...]
        else:
            for k, at in enumerate(order):
                start = pl.multiple_of((here ^ at) * chunk, chunk)
                rel_ref[pl.ds(k * chunk, chunk), :] = o_ref[pl.ds(start, chunk), :]

    anywhere = pl.BlockSpec(memory_space=pl.ANY)
    whole = pl.BlockSpec(memory_space=pltpu.VMEM)
    tall = jax.ShapeDtypeStruct((length, cols), BF)
    return pl.pallas_call(
        kernel,
        out_shape=[
            jax.ShapeDtypeStruct((length, width), BF),
            tall,
            tall,
            tall,
            tall,
            tall,
            jax.ShapeDtypeStruct((length, 128), F4),
        ],
        in_specs=[pl.BlockSpec(memory_space=pltpu.SMEM)] + [anywhere] * (count + 1) + [whole] * 6,
        out_specs=[whole] * 7,
        scratch_shapes=[
            pltpu.VMEM((width, three), BF),
            pltpu.SemaphoreType.DMA((count + line * plane,)),
        ],
        compiler_params=pltpu.CompilerParams(vmem_limit_bytes=VMEM_BYTES),
        cost_estimate=busy(17),
        name="attend",
    )(place, *[piece for piece, _, _ in pieces], qkv_line, gain, shift, bias, *tables)


def attend_back(place, pieces, out_here, q, k, v, lse, tables, order, chunk):
    length, cols = q.shape
    width = out_here.shape[1]
    heads = cols // HD
    count = len(pieces)
    block = min(BLOCK, length)
    score_scale = HD ** (-0.5)

    def kernel(place_ref, *refs):
        piece_refs = refs[:count]
        out_ref, q_ref, k_ref, v_ref, lse_ref, plain_ref, ahead_ref, behind_ref = refs[
            count : count + 8
        ]
        d_ref, all_ref, rel_ref, sum_ref, do_ref, delta_ref, dq_ref, dk_ref, sems = refs[count + 8 :]
        here = place_ref[0]
        starts = piece_rows(here, pieces, chunk)
        copy_all(
            [(ref, d_ref.at[pl.ds(at, ref.shape[0])]) for ref, at in zip(piece_refs, starts)], sems
        )

        def project(i, carry):
            rows = pl.ds(pl.multiple_of(i * block, block), block)
            do_ref[rows, :] = kernel_dot(d_ref[rows, :], out_ref[...], NT).astype(BF)
            return carry

        lax.fori_loop(0, length // block, project, 0)
        for i in range(length // block):
            rows = slice(i * block, (i + 1) * block)
            seen = (i + 1) * block
            q_rows, do_rows = q_ref[rows, :], do_ref[rows, :]
            k_rows, v_rows = k_ref[:seen, :], v_ref[:seen, :]
            allowed = (
                lax.broadcasted_iota(jnp.int32, (block, seen), 1)
                <= lax.broadcasted_iota(jnp.int32, (block, seen), 0) + i * block
            )
            found = jnp.zeros((block, cols), F4)
            deltas = jnp.zeros((block, 128), F4)
            for h in range(heads):
                mine = head_lanes((block, cols), h)
                none = jnp.zeros_like(q_rows)
                scores = kernel_dot(jnp.where(mine, q_rows, none), k_rows, NT) * score_scale
                probs = jnp.where(allowed, jnp.exp(scores - lse_ref[rows, h : h + 1]), 0.0)
                d_probs = kernel_dot(jnp.where(mine, do_rows, none), v_rows, NT)
                delta = jnp.sum(probs * d_probs, axis=1, keepdims=True)
                d_scores = (probs * (d_probs - delta)).astype(BF)
                found = jnp.where(mine, kernel_dot(d_scores, k_rows, NN), found)
                lane = lax.broadcasted_iota(jnp.int32, (block, 128), 1)
                deltas = jnp.where(lane == h, delta, deltas)
            dq_ref[rows, :] = (found * score_scale).astype(BF)
            delta_ref[rows, :] = deltas
        lse_rows = jnp.transpose(lse_ref[...])
        delta_rows = jnp.transpose(delta_ref[...])
        for j in range(length // block):
            rows = slice(j * block, (j + 1) * block)
            left = length - j * block
            k_rows, v_rows = k_ref[rows, :], v_ref[rows, :]
            q_rows, do_rows = q_ref[j * block :, :], do_ref[j * block :, :]
            allowed = lax.broadcasted_iota(jnp.int32, (block, left), 0) <= lax.broadcasted_iota(
                jnp.int32, (block, left), 1
            )
            keys = jnp.zeros((block, cols), F4)
            values = jnp.zeros((block, cols), F4)
            for h in range(heads):
                mine = head_lanes((block, cols), h)
                none = jnp.zeros_like(k_rows)
                scores = kernel_dot(jnp.where(mine, k_rows, none), q_rows, NT) * score_scale
                lse_row = lse_rows[h : h + 1, j * block :]
                probs = jnp.where(allowed, jnp.exp(scores - lse_row), 0.0)
                d_probs = kernel_dot(jnp.where(mine, v_rows, none), do_rows, NT)
                d_scores = (probs * (d_probs - delta_rows[h : h + 1, j * block :])).astype(BF)
                keys = jnp.where(mine, kernel_dot(d_scores, q_rows, NN), keys)
                values = jnp.where(mine, kernel_dot(probs.astype(BF), do_rows, NN), values)
            dk_ref[rows, :] = (keys * score_scale).astype(BF)
            all_ref[rows, 2 * cols :] = values.astype(BF)

        sum_ref[...] = jnp.zeros_like(sum_ref)

        def finish(i, carry):
            rows = pl.ds(pl.multiple_of(i * block, block), block)
            factors = (plain_ref[rows, :], ahead_ref[rows, :], behind_ref[rows, :])
            all_ref[rows, :cols] = turned(dq_ref[rows, :].astype(F4), factors, True).astype(BF)
            all_ref[rows, cols : 2 * cols] = turned(
                dk_ref[rows, :].astype(F4), factors, True
            ).astype(BF)
            sum_ref[...] += jnp.sum(all_ref[rows, :].astype(F4), axis=0, keepdims=True)
            return carry

        lax.fori_loop(0, length // block, finish, 0)
        if order is None:
            rel_ref[...] = all_ref[...]
        else:
            for n, at in enumerate(order):
                start = pl.multiple_of((here ^ at) * chunk, chunk)
                rel_ref[pl.ds(n * chunk, chunk), :] = all_ref[pl.ds(start, chunk), :]

    anywhere = pl.BlockSpec(memory_space=pl.ANY)
    whole = pl.BlockSpec(memory_space=pltpu.VMEM)
    wide = jax.ShapeDtypeStruct((length, 3 * cols), BF)
    return pl.pallas_call(
        kernel,
        out_shape=[
            jax.ShapeDtypeStruct((length, width), BF),
            wide,
            wide,
            jax.ShapeDtypeStruct((1, 3 * cols), F4),
        ],
        in_specs=[pl.BlockSpec(memory_space=pltpu.SMEM)] + [anywhere] * count + [whole] * 8,
        out_specs=[whole] * 4,
        scratch_shapes=[
            pltpu.VMEM((length, cols), BF),
            pltpu.VMEM((length, 128), F4),
            pltpu.VMEM((length, cols), BF),
            pltpu.VMEM((length, cols), BF),
            pltpu.SemaphoreType.DMA((count,)),
        ],
        compiler_params=pltpu.CompilerParams(vmem_limit_bytes=VMEM_BYTES),
        cost_estimate=busy(26),
        name="attend_back",
    )(place, *[piece for piece, _, _ in pieces], out_here, q, k, v, lse, *tables)


def outer_rows(left, pieces):
    count = len(pieces)
    starts, length = [], 0
    for piece in pieces:
        starts.append(length)
        length += piece.shape[0]
    cols, width = left.shape[1], pieces[0].shape[1]

    def kernel(left_ref, *refs):
        held, sems = refs[count + 1 :]
        copy_all(
            [(ref, held.at[pl.ds(at, ref.shape[0])]) for ref, at in zip(refs[:count], starts)], sems
        )
        refs[count][...] = kernel_dot(left_ref[...], held[...], ((0,), (0,))).astype(BF)

    anywhere = pl.BlockSpec(memory_space=pl.ANY)
    whole = pl.BlockSpec(memory_space=pltpu.VMEM)
    return pl.pallas_call(
        kernel,
        out_shape=jax.ShapeDtypeStruct((cols, width), BF),
        in_specs=[whole] + [anywhere] * count,
        out_specs=whole,
        scratch_shapes=[pltpu.VMEM((length, width), BF), pltpu.SemaphoreType.DMA((count,))],
        compiler_params=pltpu.CompilerParams(vmem_limit_bytes=VMEM_BYTES),
        cost_estimate=busy(4),
        name="outer_rows",
    )(left, *pieces)


def feed(pieces, grads, ff_line):
    line, plane, shard, both = ff_line.shape
    cols = both // 2
    width = line * plane * shard
    count = len(pieces)
    starts, length = [], 0
    for piece in pieces:
        starts.append(length)
        length += piece.shape[0]
    block = min(512, length)
    copies = 2 * count + line * plane

    def kernel(*refs):
        piece_refs, grad_refs = refs[:count], refs[count : 2 * count]
        ff_ref = refs[2 * count]
        n_ref, g_ref, a_ref, both_ref, w_held, sems = refs[2 * count + 1 :]
        pairs = []
        for f in range(line):
            for s in range(plane):
                pairs.append((ff_ref.at[f, s], w_held.at[pl.ds((s * line + f) * shard, shard)]))
        for held, found in ((n_ref, piece_refs), (g_ref, grad_refs)):
            for ref, at in zip(found, starts):
                pairs.append((ref, held.at[pl.ds(at, ref.shape[0])]))
        copy_all(pairs, sems)

        def step(i, carry):
            rows = pl.ds(pl.multiple_of(i * block, block), block)
            gate_up = kernel_dot(n_ref[rows, :], w_held[...], NN)
            both_ref[rows, :] = gate_up
            gate, up = gate_up[:, :cols], gate_up[:, cols:]
            a_ref[rows, :] = (gate / (1.0 + jnp.exp(-gate)) * up).astype(BF)
            return carry

        lax.fori_loop(0, length // block, step, 0)

    anywhere = pl.BlockSpec(memory_space=pl.ANY)
    whole = pl.BlockSpec(memory_space=pltpu.VMEM)
    return pl.pallas_call(
        kernel,
        out_shape=[
            jax.ShapeDtypeStruct((length, width), BF),
            jax.ShapeDtypeStruct((length, width), BF),
            jax.ShapeDtypeStruct((length, cols), BF),
            jax.ShapeDtypeStruct((length, both), F4),
        ],
        in_specs=[anywhere] * (2 * count + 1),
        out_specs=[whole] * 4,
        scratch_shapes=[pltpu.VMEM((width, both), BF), pltpu.SemaphoreType.DMA((copies,))],
        compiler_params=pltpu.CompilerParams(vmem_limit_bytes=VMEM_BYTES),
        cost_estimate=busy(17),
        name="feed",
    )(*pieces, *grads, ff_line)


def feed_back(grad_rows, gate_up, ff_line, down_here):
    line, plane, shard, both = ff_line.shape
    cols = both // 2
    length, width = grad_rows.shape
    half = length // 2
    block = min(512, half)

    def kernel(g_ref, both_ref, ff_ref, down_ref, d_ref, send_ref, keep_ref, w_held, sems):
        pairs = []
        for f in range(line):
            for s in range(plane):
                pairs.append((ff_ref.at[f, s], w_held.at[pl.ds((s * line + f) * shard, shard)]))
        copies = [pltpu.make_async_copy(a, b, sems.at[i]) for i, (a, b) in enumerate(pairs)]
        for copy in copies:
            copy.start()

        def step(i, carry):
            rows = pl.ds(pl.multiple_of(i * block, block), block)
            d_hidden = kernel_dot(g_ref[rows, :], down_ref[...], NT)
            gate, up = both_ref[rows, :cols], both_ref[rows, cols:]
            sigmoid = 1.0 / (1.0 + jnp.exp(-gate))
            d_gate = d_hidden * up * sigmoid * (1.0 + gate * (1.0 - sigmoid))
            d_ref[rows, :] = jnp.concatenate([d_gate, d_hidden * gate * sigmoid], 1).astype(BF)
            return carry

        lax.fori_loop(0, length // block, step, 0)
        for copy in copies:
            copy.wait()

        def back(i, carry):
            rows = pl.ds(pl.multiple_of(i * block, block), block)
            there = pl.ds(pl.multiple_of(half + i * block, block), block)
            send_ref[rows, :] = kernel_dot(d_ref[there, :], w_held[...], NT).astype(BF)
            keep_ref[rows, :] = kernel_dot(d_ref[rows, :], w_held[...], NT)
            return carry

        lax.fori_loop(0, half // block, back, 0)

    anywhere = pl.BlockSpec(memory_space=pl.ANY)
    whole = pl.BlockSpec(memory_space=pltpu.VMEM)
    return pl.pallas_call(
        kernel,
        out_shape=[
            jax.ShapeDtypeStruct((length, both), BF),
            jax.ShapeDtypeStruct((half, width), BF),
            jax.ShapeDtypeStruct((half, width), F4),
        ],
        in_specs=[whole, whole, anywhere, whole],
        out_specs=[whole] * 3,
        scratch_shapes=[
            pltpu.VMEM((width, both), BF),
            pltpu.SemaphoreType.DMA((line * plane,)),
        ],
        compiler_params=pltpu.CompilerParams(vmem_limit_bytes=VMEM_BYTES),
        cost_estimate=busy(17),
        name="feed_back",
    )(grad_rows, gate_up, ff_line, down_here)


def nothing(*refs):
    pass


def turn(values, *earlier):
    anywhere = pl.BlockSpec(memory_space=pl.ANY)
    return pl.pallas_call(
        nothing,
        out_shape=[jax.ShapeDtypeStruct(v.shape, v.dtype) for v in values],
        in_specs=[anywhere] * (len(values) + len(earlier)),
        out_specs=[anywhere] * len(values),
        input_output_aliases={i: i for i in range(len(values))},
        cost_estimate=pl.CostEstimate(flops=0, bytes_accessed=0, transcendentals=0),
        name="in_turn",
    )(*values, *earlier)


def after(values, *earlier):
    return turn([values], *earlier)[0]


def pair_columns(gate, up, lists):
    rows, width = gate.shape
    part = width // sum(len(blocks) for blocks in lists)

    def kernel(gate_ref, up_ref, blocks_ref):
        whole = [gate_ref[...].astype(F4), up_ref[...].astype(F4)]
        for i, blocks in enumerate(lists):
            columns = [w[:, at * part : (at + 1) * part] for w in whole for at in blocks]
            blocks_ref[i] = jnp.concatenate(columns, 1).astype(BF)

    held = 2 * part * len(lists[0])
    return pl.pallas_call(
        kernel,
        out_shape=jax.ShapeDtypeStruct((len(lists), rows, held), BF),
        compiler_params=pltpu.CompilerParams(vmem_limit_bytes=32 << 20),
        name="pair_columns",
    )(gate, up)


def part_columns(blocks, lists):
    parts, rows, held = blocks.shape
    count = len(lists[0])
    part = held // (2 * count)
    width = parts * count * part
    place = {at: (i, j) for i, each in enumerate(lists) for j, at in enumerate(each)}

    def kernel(blocks_ref, first_ref, second_ref):
        whole = [blocks_ref[i].astype(F4) for i in range(parts)]
        for k, ref in enumerate((first_ref, second_ref)):
            columns = []
            for at in range(parts * count):
                i, j = place[at]
                start = (k * count + j) * part
                columns.append(whole[i][:, start : start + part])
            ref[...] = jnp.concatenate(columns, 1)

    return pl.pallas_call(
        kernel,
        out_shape=[jax.ShapeDtypeStruct((rows, width), F4)] * 2,
        compiler_params=pltpu.CompilerParams(vmem_limit_bytes=32 << 20),
        name="part_columns",
    )(blocks)


def pick_columns(weight, lists):
    rows, width = weight.shape
    part = width // sum(len(blocks) for blocks in lists)

    def kernel(weight_ref, blocks_ref):
        whole = weight_ref[...].astype(F4)
        for i, blocks in enumerate(lists):
            columns = [whole[:, at * part : (at + 1) * part] for at in blocks]
            blocks_ref[i] = jnp.concatenate(columns, 1).astype(BF)

    return pl.pallas_call(
        kernel,
        out_shape=jax.ShapeDtypeStruct((len(lists), rows, part * len(lists[0])), BF),
        compiler_params=pltpu.CompilerParams(vmem_limit_bytes=32 << 20),
        name="pick_columns",
    )(weight)


def place_columns(blocks, lists):
    parts, rows, held = blocks.shape
    count = len(lists[0])
    part = held // count
    place = {at: (i, j) for i, each in enumerate(lists) for j, at in enumerate(each)}

    def kernel(blocks_ref, whole_ref):
        whole = [blocks_ref[i].astype(F4) for i in range(parts)]
        columns = []
        for at in range(parts * count):
            i, j = place[at]
            columns.append(whole[i][:, j * part : (j + 1) * part])
        whole_ref[...] = jnp.concatenate(columns, 1)

    return pl.pallas_call(
        kernel,
        out_shape=jax.ShapeDtypeStruct((rows, parts * held), F4),
        compiler_params=pltpu.CompilerParams(vmem_limit_bytes=32 << 20),
        name="place_columns",
    )(blocks)


class Links:
    def __init__(self):
        self.ns = lax.axis_size("seq")
        self.nz = lax.axis_size("fsdp")
        self.s = lax.axis_index("seq")
        self.z = lax.axis_index("fsdp")
        self.core = self.s % 2
        self.fast_plane = self.ns == 8
        self.order = [0, 2, 4, 6, 1, 3, 5, 7]

    def flip(self, values, bit):
        return lax.ppermute(values, "seq", [(i, i ^ bit) for i in range(self.ns)])

    def swap_core(self, values):
        return self.flip(values, 1)

    def hop(self, values, pairs):
        return lax.ppermute(values, "fsdp", pairs)

    def along_x(self, values):
        return self.flip(values, 2)

    def along_y(self, values):
        return self.flip(values, 4)

    def square_gather(self, own, one, two, codes):
        cut = own.shape[0] // 32 * 16
        first = one(own)
        second = two(own)
        return [
            (own, 0, 0),
            (first, codes[0], 0),
            (second, codes[1], 0),
            (two(first[:cut]), codes[0] | codes[1], 0),
            (one(second[cut:]), codes[0] | codes[1], cut),
        ]

    def with_core(self, found):
        return found + [(self.swap_core(part), at | 1, start) for part, at, start in found]

    def square_reduce(self, own, first, second, far, one, two):
        return self.square_reduce_end(
            self.square_reduce_start(own, first, second, far, one, two), one, two
        )

    def square_reduce_start(self, own, first, second, far, one, two):
        cut = far.shape[0] // 32 * 16
        far = far.astype(BF)
        via_one = one(far[:cut])
        via_two = two(far[cut:])
        second = jnp.concatenate([second[:cut] + via_one.astype(F4), second[cut:]], 0).astype(BF)
        first = jnp.concatenate([first[:cut], first[cut:] + via_two.astype(F4)], 0).astype(BF)
        return [own, first, second]

    def square_reduce_end(self, parts, one, two):
        own, first, second = parts
        return own + one(first).astype(F4) + two(second).astype(F4)

    def core_sum(self, keep, send, *earlier):
        other = self.swap_core(send.astype(BF))
        return keep + (after(other, *earlier) if earlier else other).astype(F4)

    def plane_gather(self, own):
        if not self.fast_plane:
            return [(lax.all_gather(own, "seq", axis=0, tiled=True), None, 0)]
        return self.with_core(self.square_gather(own, self.along_x, self.along_y, (2, 4)))

    def plane_reduce(self, keep, send):
        if not self.fast_plane:
            terms = jnp.concatenate([keep, send], 0).astype(BF)
            return lax.psum_scatter(terms, "seq", scatter_dimension=0, tiled=True).astype(F4)
        pair = self.core_sum(keep, send)
        rows = pair.shape[0] // 4
        terms = [pair[i * rows : (i + 1) * rows] for i in range(4)]
        return self.square_reduce(*terms, self.along_x, self.along_y)

    def line_gather(self, own):
        return lax.all_gather(own, "fsdp", axis=0, tiled=True)

    def line_reduce(self, terms):
        return lax.psum_scatter(terms, "fsdp", scatter_dimension=0, tiled=True)

    def swap_blocks(self, blocks):
        return lax.all_to_all(blocks, "seq", split_axis=0, concat_axis=0, tiled=True)

    def rows_sorted(self, blocks):
        return blocks.transpose(1, 0, 2, 3).reshape(-1, blocks.shape[3])

    def rows_by_line(self, rows_in, shard_rows):
        shape = (self.ns, self.nz, shard_rows, rows_in.shape[1])
        return rows_in.reshape(shape).transpose(1, 0, 2, 3)

    def ff_lists(self):
        return [[s * self.nz + f for f in range(self.nz)] for s in range(self.ns)]

    def short_gather_line(self, own):
        held = own[None, :]
        for k in range(1, self.nz):
            other = lax.ppermute(own, "fsdp", [(i, i ^ k) for i in range(self.nz)])
            held = jnp.concatenate([held, other[None, :]], 0)
        bit = 1
        while bit < self.nz:
            pairs = held.reshape(-1, 2, bit, own.shape[0])
            held = jnp.where((self.z & bit) != 0, pairs[:, ::-1], pairs).reshape(held.shape)
            bit *= 2
        return held

    def short_gather_plane(self, held):
        bit = 1
        while bit < self.ns:
            other = self.flip(held, bit)
            high = (self.s & bit) != 0
            first = jnp.where(high, other, held)
            second = jnp.where(high, held, other)
            held = jnp.concatenate([first, second], 0)
            bit *= 2
        return held

    def short_reduce(self, held):
        bit = self.ns // 2
        while bit:
            half = held.shape[0] // 2
            high = (self.s & bit) != 0
            keep = jnp.where(high, held[half:], held[:half])
            send = jnp.where(high, held[:half], held[half:])
            held = keep + self.flip(send, bit)
            bit //= 2
        total = lax.dynamic_index_in_dim(held, self.z, 0, keepdims=False)
        for k in range(1, self.nz):
            send = lax.dynamic_index_in_dim(held, self.z ^ k, 0, keepdims=False)
            total = total + lax.ppermute(send, "fsdp", [(i, i ^ k) for i in range(self.nz)])
        return total


def on_device(
    hidden_in,
    positions,
    norm1_gain,
    norm1_shift,
    w_qkv,
    b_qkv,
    w_out,
    norm2_gain,
    norm2_shift,
    w_gate,
    w_up,
    w_down,
    grad_out,
):
    links = Links()
    ns, nz = links.ns, links.nz
    devices = ns * nz
    tok_rows = hidden_in.shape[1]
    width = hidden_in.shape[2]
    shard_rows = w_qkv.shape[0]
    seq_places = positions[0]
    length = seq_places.shape[0]
    cols = width // ns
    score_scale = HD ** (-0.5)

    lists = links.ff_lists()
    out_here = links.line_gather(w_out)
    short = jnp.concatenate([norm1_gain, norm1_shift, norm2_gain, norm2_shift, b_qkv])
    short_line = links.short_gather_line(short)
    qkv_lists = [[s, ns + s, 2 * ns + s] for s in range(ns)]
    qkv_blocks = links.swap_blocks(pick_columns(w_qkv, qkv_lists))
    qkv_blocks, short_line = turn([qkv_blocks, short_line], out_here)
    qkv_line = links.line_gather(qkv_blocks[None])
    ff_blocks = links.swap_blocks(pair_columns(w_gate, w_up, lists))

    short_all = links.short_gather_plane(short_line)
    short_all, w_down = turn([short_all, w_down])
    n = shard_rows
    first_gain = short_all[:, :n].reshape(-1)
    first_shift = short_all[:, n : 2 * n].reshape(-1)
    second_gain = short_all[:, 2 * n : 3 * n].reshape(-1)
    second_shift = short_all[:, 3 * n : 4 * n].reshape(-1)
    bias_all = short_all[:, 4 * n :].reshape(3, ns, cols)
    bias_here = lax.dynamic_index_in_dim(bias_all, links.s, 1, keepdims=False).reshape(3 * cols)

    place = jnp.stack([links.s, links.z]).astype(jnp.int32)
    order = links.order if links.fast_plane else None
    inputs = hidden_in.reshape(tok_rows, width).astype(F4)
    _, first_hat, first_inverse = layer_norm(inputs, first_gain, first_shift)
    first_pieces = links.plane_gather(hidden_in.reshape(tok_rows, width))
    cotangent_low = grad_out.reshape(tok_rows, width)
    tables = rotary_tables(seq_places, cols)
    half = length // 2

    def let(values, *earlier):
        flat = turn([v for group in values for v in group], *earlier)
        found = []
        for group in values:
            found.append(list(flat[: len(group)]))
            flat = flat[len(group) :]
        return found

    def arrays(pieces):
        return [piece for piece, _, _ in pieces]

    def renewed(pieces, values):
        return [(value, at, start) for value, (_, at, start) in zip(values, pieces)]

    vectors = [v.astype(F4)[None] for v in (first_gain, first_shift, bias_here)]
    found, vectors, (ff_blocks, cotangent_low) = let(
        [arrays(first_pieces), vectors, [ff_blocks, cotangent_low]]
    )
    found, vectors, (ff_blocks, cotangent_low) = let(
        [found, vectors, [ff_blocks, cotangent_low]], qkv_line
    )
    first_pieces = renewed(first_pieces, found)
    ff_line = links.line_gather(ff_blocks[None])
    down_here = links.line_gather(w_down)
    cotangent_pieces = arrays(links.plane_gather(cotangent_low))
    normed_rows, queries, keys, values, mixed, mixed_rel, log_totals = attend(
        place,
        first_pieces,
        vectors[0],
        vectors[1],
        qkv_line,
        vectors[2],
        tables,
        order,
        tok_rows,
    )
    out_send = dot(mixed_rel[half:], out_here, BF)
    out_keep = dot(mixed_rel[:half], out_here)
    middle = inputs + links.plane_reduce(out_keep, out_send)

    second_normed, second_hat, second_inverse = layer_norm(middle, second_gain, second_shift)
    second_low = second_normed.astype(BF)
    second_pieces = arrays(links.plane_gather(second_low))
    second_rows, cotangent_rows, hidden_mid, gate_up = feed(
        second_pieces, cotangent_pieces, ff_line
    )
    down_grad = dot_tn(hidden_mid, cotangent_rows).astype(BF)
    down_sum = links.line_reduce(down_grad)
    grad_rows, gate_up = turn([cotangent_rows, gate_up], down_grad)
    d_ff, second_send, second_keep = feed_back(grad_rows, gate_up, ff_line, down_here)
    ff_grad = links.rows_by_line(dot_tn(second_rows, d_ff).astype(BF), shard_rows)
    ff_sum = links.line_reduce(after(ff_grad, down_sum)).reshape(ns, shard_rows, -1)
    second_send, second_keep = turn([second_send, second_keep], ff_grad)
    d_second = links.plane_reduce(second_keep, second_send)
    d_second = after(d_second, down_sum)
    d_from_norm, second_gain_grad, second_shift_grad = norm_backward(
        d_second, second_hat, second_inverse, second_gain
    )
    d_middle = cotangent_low.astype(F4) + d_from_norm
    d_middle_pieces = links.plane_gather(d_middle.astype(BF))
    out_grad = outer_rows(mixed_rel, arrays(d_middle_pieces))
    d_middle_rows, d_projected, d_projected_rel, bias_grad = attend_back(
        place,
        d_middle_pieces,
        out_here,
        queries,
        keys,
        values,
        log_totals,
        tables,
        order,
        tok_rows,
    )
    qkv_here = links.rows_sorted(qkv_line)
    first_send = dot_nt(d_projected_rel[half:], qkv_here).astype(BF)
    d_projected = after(d_projected, first_send)
    qkv_grad = links.rows_by_line(dot_tn(normed_rows, d_projected).astype(BF), shard_rows)
    qkv_sum = links.line_reduce(after(qkv_grad, ff_sum))
    ff_swapped = links.swap_blocks(ff_sum)
    out_share = links.line_reduce(after(out_grad, qkv_sum, ff_swapped))
    qkv_sum = qkv_sum.reshape(ns, shard_rows, -1)
    bias_grad = bias_grad.reshape(3, 1, cols)

    hidden_later = after(hidden_mid, d_middle_rows)
    layer_send = dot(hidden_later[half:], down_here, BF)
    layer_keep = dot(hidden_later[:half], down_here)
    layer_out = (middle + links.plane_reduce(layer_keep, layer_send)).astype(BF)

    first_keep = dot_nt(d_projected_rel[:half], qkv_here)
    d_first = links.plane_reduce(first_keep, first_send)
    d_from_first, first_gain_grad, first_shift_grad = norm_backward(
        d_first, first_hat, first_inverse, first_gain
    )
    grad_in = (d_middle + d_from_first).astype(BF).reshape(1, tok_rows, width)

    placed = lax.dynamic_update_slice(
        jnp.zeros((3, ns, cols), F4), bias_grad, (0, links.s, 0)
    ).reshape(devices, -1)
    short_terms = jnp.concatenate(
        [
            first_gain_grad.reshape(devices, n),
            first_shift_grad.reshape(devices, n),
            second_gain_grad.reshape(devices, n),
            second_shift_grad.reshape(devices, n),
            placed,
        ],
        1,
    )
    short_sums = links.short_reduce(short_terms)

    gate_share, up_share = part_columns(ff_swapped, lists)
    qkv_share = place_columns(links.swap_blocks(qkv_sum), qkv_lists)
    return (
        layer_out.reshape(1, tok_rows, width),
        grad_in,
        short_sums[:n],
        short_sums[n : 2 * n],
        qkv_share,
        short_sums[4 * n :],
        out_share.astype(F4),
        short_sums[2 * n : 3 * n],
        short_sums[3 * n : 4 * n],
        gate_share,
        up_share,
        down_sum.astype(F4),
    )


def solution(mesh):
    both = ("seq", "fsdp")
    rows = P("fsdp", "seq", None)
    vector = P(both)
    matrix = P(both, None)
    return jax.shard_map(
        on_device,
        mesh=mesh,
        in_specs=(
            rows,
            P("fsdp", None),
            vector,
            vector,
            matrix,
            vector,
            matrix,
            vector,
            vector,
            matrix,
            matrix,
            matrix,
            rows,
        ),
        out_specs=(
            rows,
            rows,
            vector,
            vector,
            matrix,
            vector,
            matrix,
            vector,
            vector,
            matrix,
            matrix,
            matrix,
        ),
        check_vma=False,
    )
```

```python
import jax
import jax.numpy as jnp
from jax import lax
from jax.experimental import pallas as pl
from jax.experimental.pallas import tpu as pltpu
from jax.sharding import PartitionSpec as P

HD = 64
ROT = 16

EPS = 1e-05
NEG = -1e30

BF = jnp.bfloat16
F4 = jnp.float32


def dot(a, b, out=F4):
    return jnp.dot(a, b, preferred_element_type=F4).astype(out)


def dot_nt(a, b):
    return lax.dot_general(a, b, (((1,), (1,)), ((), ())), preferred_element_type=F4)


def dot_tn(a, b):
    return lax.dot_general(a, b, (((0,), (0,)), ((), ())), preferred_element_type=F4)


def layer_norm(values, gain_row, shift_row):
    row_mean = jnp.mean(values, axis=1, keepdims=True)
    centred = values - row_mean
    inverse = lax.rsqrt(jnp.mean(centred * centred, axis=1, keepdims=True) + EPS)
    normed = centred * inverse
    return (normed * gain_row.astype(F4) + shift_row.astype(F4), normed, inverse)


def norm_backward(grad_rows, normed, inverse, gain_row):
    scaled = grad_rows * gain_row.astype(F4)
    inner_term = (
        scaled
        - jnp.mean(scaled, axis=1, keepdims=True)
        - normed * jnp.mean(scaled * normed, axis=1, keepdims=True)
    )
    return (inner_term * inverse, jnp.sum(grad_rows * normed, axis=0), jnp.sum(grad_rows, axis=0))


def angle_tables(places):
    half_rot = ROT // 2
    frequency = 10000.0 ** (-2.0 * jnp.arange(half_rot, dtype=F4) / ROT)
    angles = places.astype(F4)[:, None] * frequency[None, :]
    return (
        jnp.concatenate([jnp.cos(angles), jnp.cos(angles)], 1),
        jnp.concatenate([jnp.sin(angles), jnp.sin(angles)], 1),
    )


def busy(microseconds):
    return pl.CostEstimate(
        flops=int(microseconds * 1e9), bytes_accessed=0, transcendentals=0
    )


VMEM_BYTES = 56 << 20
BLOCK = 256


def kernel_dot(a, b, contract):
    return lax.dot_general(a, b, (contract, ((), ())), preferred_element_type=F4)


NN = ((1,), (0,))
NT = ((1,), (1,))


def copy_all(pairs, sems):
    copies = [pltpu.make_async_copy(a, b, sems.at[i]) for i, (a, b) in enumerate(pairs)]
    for copy in copies:
        copy.start()
    for copy in copies:
        copy.wait()


def piece_rows(place, pieces, chunk):
    return [
        0 if at is None else pl.multiple_of((place ^ at) * chunk + start, 16)
        for _, at, start in pieces
    ]


def turned(rows, tables, backward):
    plain, ahead, behind = tables
    width = rows.shape[1]
    half = ROT // 2
    moved = pltpu.roll(rows, width - half, 1) * ahead + pltpu.roll(rows, half, 1) * behind
    return rows * plain - moved if backward else rows * plain + moved


def rotary_tables(places, cols):
    half = ROT // 2
    cosine, sine = angle_tables(places)
    rows = places.shape[0]
    rest = jnp.zeros((rows, HD - ROT), F4)
    none = jnp.zeros((rows, half), F4)
    plain = jnp.concatenate([cosine, rest + 1.0], 1)
    ahead = jnp.concatenate([-sine[:, :half], none, rest], 1)
    behind = jnp.concatenate([none, sine[:, half:], rest], 1)
    return [jnp.tile(table, (1, cols // HD)) for table in (plain, ahead, behind)]


def head_lanes(shape, head):
    return lax.broadcasted_iota(jnp.int32, shape, 1) // HD == head


def attend(place, pieces, gain, shift, qkv_line, bias, tables, order, chunk):
    line, plane, shard, three = qkv_line.shape
    cols = three // 3
    width = line * plane * shard
    length = tables[0].shape[0]
    heads = cols // HD
    count = len(pieces)
    block = min(BLOCK, length)
    score_scale = HD ** (-0.5)

    def kernel(place_ref, *refs):
        piece_refs = refs[:count]
        w_ref, gain_ref, shift_ref, bias_ref, plain_ref, ahead_ref, behind_ref = refs[
            count : count + 7
        ]
        n_ref, q_ref, k_ref, v_ref, o_ref, rel_ref, lse_ref, w_held, sems = refs[count + 7 :]
        here = place_ref[0]
        starts = piece_rows(here, pieces, chunk)
        pairs = [
            (ref, n_ref.at[pl.ds(at, ref.shape[0])]) for ref, at in zip(piece_refs, starts)
        ]
        for f in range(line):
            for s in range(plane):
                pairs.append((w_ref.at[f, s], w_held.at[pl.ds((s * line + f) * shard, shard)]))
        copy_all(pairs, sems)

        def project(i, carry):
            rows = pl.ds(pl.multiple_of(i * block, block), block)
            raw = n_ref[rows, :].astype(F4)
            centred = raw - jnp.mean(raw, axis=1, keepdims=True)
            inverse = lax.rsqrt(jnp.mean(centred * centred, axis=1, keepdims=True) + EPS)
            normed = (centred * inverse * gain_ref[...] + shift_ref[...]).astype(BF)
            n_ref[rows, :] = normed
            found = kernel_dot(normed, w_held[...], NN) + bias_ref[...]
            factors = (plain_ref[rows, :], ahead_ref[rows, :], behind_ref[rows, :])
            q_ref[rows, :] = turned(found[:, :cols], factors, False).astype(BF)
            k_ref[rows, :] = turned(found[:, cols : 2 * cols], factors, False).astype(BF)
            v_ref[rows, :] = found[:, 2 * cols :].astype(BF)
            return carry

        lax.fori_loop(0, length // block, project, 0)
        for i in range(length // block):
            rows = slice(i * block, (i + 1) * block)
            seen = (i + 1) * block
            q_rows = q_ref[rows, :]
            k_rows = k_ref[:seen, :]
            v_rows = v_ref[:seen, :]
            allowed = (
                lax.broadcasted_iota(jnp.int32, (block, seen), 1)
                <= lax.broadcasted_iota(jnp.int32, (block, seen), 0) + i * block
            )
            found = jnp.zeros((block, cols), F4)
            totals = jnp.zeros((block, 128), F4)
            for h in range(heads):
                mine = head_lanes((block, cols), h)
                scores = kernel_dot(jnp.where(mine, q_rows, jnp.zeros_like(q_rows)), k_rows, NT)
                scores = jnp.where(allowed, scores * score_scale, NEG)
                peak = jnp.max(scores, axis=1, keepdims=True)
                weights = jnp.exp(scores - peak)
                total = jnp.sum(weights, axis=1, keepdims=True)
                weights = (weights * (1.0 / total)).astype(BF)
                found = jnp.where(mine, kernel_dot(weights, v_rows, NN), found)
                lane = lax.broadcasted_iota(jnp.int32, (block, 128), 1)
                totals = jnp.where(lane == h, peak + jnp.log(total), totals)
            o_ref[rows, :] = found.astype(BF)
            lse_ref[rows, :] = totals
        if order is None:
            rel_ref[...] = o_ref[...]
        else:
            for k, at in enumerate(order):
                start = pl.multiple_of((here ^ at) * chunk, chunk)
                rel_ref[pl.ds(k * chunk, chunk), :] = o_ref[pl.ds(start, chunk), :]

    anywhere = pl.BlockSpec(memory_space=pl.ANY)
    whole = pl.BlockSpec(memory_space=pltpu.VMEM)
    tall = jax.ShapeDtypeStruct((length, cols), BF)
    return pl.pallas_call(
        kernel,
        out_shape=[
            jax.ShapeDtypeStruct((length, width), BF),
            tall,
            tall,
            tall,
            tall,
            tall,
            jax.ShapeDtypeStruct((length, 128), F4),
        ],
        in_specs=[pl.BlockSpec(memory_space=pltpu.SMEM)] + [anywhere] * (count + 1) + [whole] * 6,
        out_specs=[whole] * 7,
        scratch_shapes=[
            pltpu.VMEM((width, three), BF),
            pltpu.SemaphoreType.DMA((count + line * plane,)),
        ],
        compiler_params=pltpu.CompilerParams(vmem_limit_bytes=VMEM_BYTES),
        cost_estimate=busy(17),
        name="attend",
    )(place, *[piece for piece, _, _ in pieces], qkv_line, gain, shift, bias, *tables)


def attend_back(place, pieces, out_here, q, k, v, lse, tables, order, chunk):
    length, cols = q.shape
    width = out_here.shape[1]
    heads = cols // HD
    count = len(pieces)
    block = min(BLOCK, length)
    score_scale = HD ** (-0.5)

    def kernel(place_ref, *refs):
        piece_refs = refs[:count]
        out_ref, q_ref, k_ref, v_ref, lse_ref, plain_ref, ahead_ref, behind_ref = refs[
            count : count + 8
        ]
        d_ref, all_ref, rel_ref, sum_ref, do_ref, delta_ref, dq_ref, dk_ref, sems = refs[count + 8 :]
        here = place_ref[0]
        starts = piece_rows(here, pieces, chunk)
        copy_all(
            [(ref, d_ref.at[pl.ds(at, ref.shape[0])]) for ref, at in zip(piece_refs, starts)], sems
        )

        def project(i, carry):
            rows = pl.ds(pl.multiple_of(i * block, block), block)
            do_ref[rows, :] = kernel_dot(d_ref[rows, :], out_ref[...], NT).astype(BF)
            return carry

        lax.fori_loop(0, length // block, project, 0)
        for i in range(length // block):
            rows = slice(i * block, (i + 1) * block)
            seen = (i + 1) * block
            q_rows, do_rows = q_ref[rows, :], do_ref[rows, :]
            k_rows, v_rows = k_ref[:seen, :], v_ref[:seen, :]
            allowed = (
                lax.broadcasted_iota(jnp.int32, (block, seen), 1)
                <= lax.broadcasted_iota(jnp.int32, (block, seen), 0) + i * block
            )
            found = jnp.zeros((block, cols), F4)
            deltas = jnp.zeros((block, 128), F4)
            for h in range(heads):
                mine = head_lanes((block, cols), h)
                none = jnp.zeros_like(q_rows)
                scores = kernel_dot(jnp.where(mine, q_rows, none), k_rows, NT) * score_scale
                probs = jnp.where(allowed, jnp.exp(scores - lse_ref[rows, h : h + 1]), 0.0)
                d_probs = kernel_dot(jnp.where(mine, do_rows, none), v_rows, NT)
                delta = jnp.sum(probs * d_probs, axis=1, keepdims=True)
                d_scores = (probs * (d_probs - delta)).astype(BF)
                found = jnp.where(mine, kernel_dot(d_scores, k_rows, NN), found)
                lane = lax.broadcasted_iota(jnp.int32, (block, 128), 1)
                deltas = jnp.where(lane == h, delta, deltas)
            dq_ref[rows, :] = (found * score_scale).astype(BF)
            delta_ref[rows, :] = deltas
        lse_rows = jnp.transpose(lse_ref[...])
        delta_rows = jnp.transpose(delta_ref[...])
        for j in range(length // block):
            rows = slice(j * block, (j + 1) * block)
            left = length - j * block
            k_rows, v_rows = k_ref[rows, :], v_ref[rows, :]
            q_rows, do_rows = q_ref[j * block :, :], do_ref[j * block :, :]
            allowed = lax.broadcasted_iota(jnp.int32, (block, left), 0) <= lax.broadcasted_iota(
                jnp.int32, (block, left), 1
            )
            keys = jnp.zeros((block, cols), F4)
            values = jnp.zeros((block, cols), F4)
            for h in range(heads):
                mine = head_lanes((block, cols), h)
                none = jnp.zeros_like(k_rows)
                scores = kernel_dot(jnp.where(mine, k_rows, none), q_rows, NT) * score_scale
                lse_row = lse_rows[h : h + 1, j * block :]
                probs = jnp.where(allowed, jnp.exp(scores - lse_row), 0.0)
                d_probs = kernel_dot(jnp.where(mine, v_rows, none), do_rows, NT)
                d_scores = (probs * (d_probs - delta_rows[h : h + 1, j * block :])).astype(BF)
                keys = jnp.where(mine, kernel_dot(d_scores, q_rows, NN), keys)
                values = jnp.where(mine, kernel_dot(probs.astype(BF), do_rows, NN), values)
            dk_ref[rows, :] = (keys * score_scale).astype(BF)
            all_ref[rows, 2 * cols :] = values.astype(BF)

        sum_ref[...] = jnp.zeros_like(sum_ref)

        def finish(i, carry):
            rows = pl.ds(pl.multiple_of(i * block, block), block)
            factors = (plain_ref[rows, :], ahead_ref[rows, :], behind_ref[rows, :])
            all_ref[rows, :cols] = turned(dq_ref[rows, :].astype(F4), factors, True).astype(BF)
            all_ref[rows, cols : 2 * cols] = turned(
                dk_ref[rows, :].astype(F4), factors, True
            ).astype(BF)
            sum_ref[...] += jnp.sum(all_ref[rows, :].astype(F4), axis=0, keepdims=True)
            return carry

        lax.fori_loop(0, length // block, finish, 0)
        if order is None:
            rel_ref[...] = all_ref[...]
        else:
            for n, at in enumerate(order):
                start = pl.multiple_of((here ^ at) * chunk, chunk)
                rel_ref[pl.ds(n * chunk, chunk), :] = all_ref[pl.ds(start, chunk), :]

    anywhere = pl.BlockSpec(memory_space=pl.ANY)
    whole = pl.BlockSpec(memory_space=pltpu.VMEM)
    wide = jax.ShapeDtypeStruct((length, 3 * cols), BF)
    return pl.pallas_call(
        kernel,
        out_shape=[
            jax.ShapeDtypeStruct((length, width), BF),
            wide,
            wide,
            jax.ShapeDtypeStruct((1, 3 * cols), F4),
        ],
        in_specs=[pl.BlockSpec(memory_space=pltpu.SMEM)] + [anywhere] * count + [whole] * 8,
        out_specs=[whole] * 4,
        scratch_shapes=[
            pltpu.VMEM((length, cols), BF),
            pltpu.VMEM((length, 128), F4),
            pltpu.VMEM((length, cols), BF),
            pltpu.VMEM((length, cols), BF),
            pltpu.SemaphoreType.DMA((count,)),
        ],
        compiler_params=pltpu.CompilerParams(vmem_limit_bytes=VMEM_BYTES),
        cost_estimate=busy(26),
        name="attend_back",
    )(place, *[piece for piece, _, _ in pieces], out_here, q, k, v, lse, *tables)


def outer_rows(left, pieces):
    count = len(pieces)
    starts, length = [], 0
    for piece in pieces:
        starts.append(length)
        length += piece.shape[0]
    cols, width = left.shape[1], pieces[0].shape[1]

    def kernel(left_ref, *refs):
        held, sems = refs[count + 1 :]
        copy_all(
            [(ref, held.at[pl.ds(at, ref.shape[0])]) for ref, at in zip(refs[:count], starts)], sems
        )
        refs[count][...] = kernel_dot(left_ref[...], held[...], ((0,), (0,))).astype(BF)

    anywhere = pl.BlockSpec(memory_space=pl.ANY)
    whole = pl.BlockSpec(memory_space=pltpu.VMEM)
    return pl.pallas_call(
        kernel,
        out_shape=jax.ShapeDtypeStruct((cols, width), BF),
        in_specs=[whole] + [anywhere] * count,
        out_specs=whole,
        scratch_shapes=[pltpu.VMEM((length, width), BF), pltpu.SemaphoreType.DMA((count,))],
        compiler_params=pltpu.CompilerParams(vmem_limit_bytes=VMEM_BYTES),
        cost_estimate=busy(4),
        name="outer_rows",
    )(left, *pieces)


def feed(pieces, grads, ff_line):
    line, plane, shard, both = ff_line.shape
    cols = both // 2
    width = line * plane * shard
    count = len(pieces)
    starts, length = [], 0
    for piece in pieces:
        starts.append(length)
        length += piece.shape[0]
    block = min(512, length)
    copies = 2 * count + line * plane

    def kernel(*refs):
        piece_refs, grad_refs = refs[:count], refs[count : 2 * count]
        ff_ref = refs[2 * count]
        n_ref, g_ref, a_ref, both_ref, w_held, sems = refs[2 * count + 1 :]
        pairs = []
        for f in range(line):
            for s in range(plane):
                pairs.append((ff_ref.at[f, s], w_held.at[pl.ds((s * line + f) * shard, shard)]))
        for held, found in ((n_ref, piece_refs), (g_ref, grad_refs)):
            for ref, at in zip(found, starts):
                pairs.append((ref, held.at[pl.ds(at, ref.shape[0])]))
        copy_all(pairs, sems)

        def step(i, carry):
            rows = pl.ds(pl.multiple_of(i * block, block), block)
            gate_up = kernel_dot(n_ref[rows, :], w_held[...], NN)
            both_ref[rows, :] = gate_up
            gate, up = gate_up[:, :cols], gate_up[:, cols:]
            a_ref[rows, :] = (gate / (1.0 + jnp.exp(-gate)) * up).astype(BF)
            return carry

        lax.fori_loop(0, length // block, step, 0)

    anywhere = pl.BlockSpec(memory_space=pl.ANY)
    whole = pl.BlockSpec(memory_space=pltpu.VMEM)
    return pl.pallas_call(
        kernel,
        out_shape=[
            jax.ShapeDtypeStruct((length, width), BF),
            jax.ShapeDtypeStruct((length, width), BF),
            jax.ShapeDtypeStruct((length, cols), BF),
            jax.ShapeDtypeStruct((length, both), F4),
        ],
        in_specs=[anywhere] * (2 * count + 1),
        out_specs=[whole] * 4,
        scratch_shapes=[pltpu.VMEM((width, both), BF), pltpu.SemaphoreType.DMA((copies,))],
        compiler_params=pltpu.CompilerParams(vmem_limit_bytes=VMEM_BYTES),
        cost_estimate=busy(17),
        name="feed",
    )(*pieces, *grads, ff_line)


def feed_back(grad_rows, gate_up, ff_line, down_here):
    line, plane, shard, both = ff_line.shape
    cols = both // 2
    length, width = grad_rows.shape
    half = length // 2
    block = min(512, half)

    def kernel(g_ref, both_ref, ff_ref, down_ref, d_ref, send_ref, keep_ref, w_held, sems):
        pairs = []
        for f in range(line):
            for s in range(plane):
                pairs.append((ff_ref.at[f, s], w_held.at[pl.ds((s * line + f) * shard, shard)]))
        copies = [pltpu.make_async_copy(a, b, sems.at[i]) for i, (a, b) in enumerate(pairs)]
        for copy in copies:
            copy.start()

        def step(i, carry):
            rows = pl.ds(pl.multiple_of(i * block, block), block)
            d_hidden = kernel_dot(g_ref[rows, :], down_ref[...], NT)
            gate, up = both_ref[rows, :cols], both_ref[rows, cols:]
            sigmoid = 1.0 / (1.0 + jnp.exp(-gate))
            d_gate = d_hidden * up * sigmoid * (1.0 + gate * (1.0 - sigmoid))
            d_ref[rows, :] = jnp.concatenate([d_gate, d_hidden * gate * sigmoid], 1).astype(BF)
            return carry

        lax.fori_loop(0, length // block, step, 0)
        for copy in copies:
            copy.wait()

        def back(i, carry):
            rows = pl.ds(pl.multiple_of(i * block, block), block)
            there = pl.ds(pl.multiple_of(half + i * block, block), block)
            send_ref[rows, :] = kernel_dot(d_ref[there, :], w_held[...], NT).astype(BF)
            keep_ref[rows, :] = kernel_dot(d_ref[rows, :], w_held[...], NT)
            return carry

        lax.fori_loop(0, half // block, back, 0)

    anywhere = pl.BlockSpec(memory_space=pl.ANY)
    whole = pl.BlockSpec(memory_space=pltpu.VMEM)
    return pl.pallas_call(
        kernel,
        out_shape=[
            jax.ShapeDtypeStruct((length, both), BF),
            jax.ShapeDtypeStruct((half, width), BF),
            jax.ShapeDtypeStruct((half, width), F4),
        ],
        in_specs=[whole, whole, anywhere, whole],
        out_specs=[whole] * 3,
        scratch_shapes=[
            pltpu.VMEM((width, both), BF),
            pltpu.SemaphoreType.DMA((line * plane,)),
        ],
        compiler_params=pltpu.CompilerParams(vmem_limit_bytes=VMEM_BYTES),
        cost_estimate=busy(17),
        name="feed_back",
    )(grad_rows, gate_up, ff_line, down_here)


def nothing(*refs):
    pass


def turn(values, *earlier):
    anywhere = pl.BlockSpec(memory_space=pl.ANY)
    return pl.pallas_call(
        nothing,
        out_shape=[jax.ShapeDtypeStruct(v.shape, v.dtype) for v in values],
        in_specs=[anywhere] * (len(values) + len(earlier)),
        out_specs=[anywhere] * len(values),
        input_output_aliases={i: i for i in range(len(values))},
        cost_estimate=pl.CostEstimate(flops=0, bytes_accessed=0, transcendentals=0),
        name="in_turn",
    )(*values, *earlier)


def after(values, *earlier):
    return turn([values], *earlier)[0]


def pair_columns(gate, up, lists):
    rows, width = gate.shape
    part = width // sum(len(blocks) for blocks in lists)

    def kernel(gate_ref, up_ref, blocks_ref):
        whole = [gate_ref[...].astype(F4), up_ref[...].astype(F4)]
        for i, blocks in enumerate(lists):
            columns = [w[:, at * part : (at + 1) * part] for w in whole for at in blocks]
            blocks_ref[i] = jnp.concatenate(columns, 1).astype(BF)

    held = 2 * part * len(lists[0])
    return pl.pallas_call(
        kernel,
        out_shape=jax.ShapeDtypeStruct((len(lists), rows, held), BF),
        compiler_params=pltpu.CompilerParams(vmem_limit_bytes=32 << 20),
        name="pair_columns",
    )(gate, up)


def part_columns(blocks, lists):
    parts, rows, held = blocks.shape
    count = len(lists[0])
    part = held // (2 * count)
    width = parts * count * part
    place = {at: (i, j) for i, each in enumerate(lists) for j, at in enumerate(each)}

    def kernel(blocks_ref, first_ref, second_ref):
        whole = [blocks_ref[i].astype(F4) for i in range(parts)]
        for k, ref in enumerate((first_ref, second_ref)):
            columns = []
            for at in range(parts * count):
                i, j = place[at]
                start = (k * count + j) * part
                columns.append(whole[i][:, start : start + part])
            ref[...] = jnp.concatenate(columns, 1)

    return pl.pallas_call(
        kernel,
        out_shape=[jax.ShapeDtypeStruct((rows, width), F4)] * 2,
        compiler_params=pltpu.CompilerParams(vmem_limit_bytes=32 << 20),
        name="part_columns",
    )(blocks)


def pick_columns(weight, lists):
    rows, width = weight.shape
    part = width // sum(len(blocks) for blocks in lists)

    def kernel(weight_ref, blocks_ref):
        whole = weight_ref[...].astype(F4)
        for i, blocks in enumerate(lists):
            columns = [whole[:, at * part : (at + 1) * part] for at in blocks]
            blocks_ref[i] = jnp.concatenate(columns, 1).astype(BF)

    return pl.pallas_call(
        kernel,
        out_shape=jax.ShapeDtypeStruct((len(lists), rows, part * len(lists[0])), BF),
        compiler_params=pltpu.CompilerParams(vmem_limit_bytes=32 << 20),
        name="pick_columns",
    )(weight)


def place_columns(blocks, lists):
    parts, rows, held = blocks.shape
    count = len(lists[0])
    part = held // count
    place = {at: (i, j) for i, each in enumerate(lists) for j, at in enumerate(each)}

    def kernel(blocks_ref, whole_ref):
        whole = [blocks_ref[i].astype(F4) for i in range(parts)]
        columns = []
        for at in range(parts * count):
            i, j = place[at]
            columns.append(whole[i][:, j * part : (j + 1) * part])
        whole_ref[...] = jnp.concatenate(columns, 1)

    return pl.pallas_call(
        kernel,
        out_shape=jax.ShapeDtypeStruct((rows, parts * held), F4),
        compiler_params=pltpu.CompilerParams(vmem_limit_bytes=32 << 20),
        name="place_columns",
    )(blocks)


class Links:
    def __init__(self):
        self.ns = lax.axis_size("seq")
        self.nz = lax.axis_size("fsdp")
        self.s = lax.axis_index("seq")
        self.z = lax.axis_index("fsdp")
        self.core = self.s % 2
        self.fast_plane = self.ns == 8
        self.order = [0, 2, 4, 6, 1, 3, 5, 7]

    def flip(self, values, bit):
        return lax.ppermute(values, "seq", [(i, i ^ bit) for i in range(self.ns)])

    def swap_core(self, values):
        return self.flip(values, 1)

    def hop(self, values, pairs):
        return lax.ppermute(values, "fsdp", pairs)

    def along_x(self, values):
        return self.flip(values, 2)

    def along_y(self, values):
        return self.flip(values, 4)

    def square_gather(self, own, one, two, codes):
        cut = own.shape[0] // 32 * 16
        first = one(own)
        second = two(own)
        return [
            (own, 0, 0),
            (first, codes[0], 0),
            (second, codes[1], 0),
            (two(first[:cut]), codes[0] | codes[1], 0),
            (one(second[cut:]), codes[0] | codes[1], cut),
        ]

    def with_core(self, found):
        return found + [(self.swap_core(part), at | 1, start) for part, at, start in found]

    def square_reduce(self, own, first, second, far, one, two):
        return self.square_reduce_end(
            self.square_reduce_start(own, first, second, far, one, two), one, two
        )

    def square_reduce_start(self, own, first, second, far, one, two):
        cut = far.shape[0] // 32 * 16
        far = far.astype(BF)
        via_one = one(far[:cut])
        via_two = two(far[cut:])
        second = jnp.concatenate([second[:cut] + via_one.astype(F4), second[cut:]], 0).astype(BF)
        first = jnp.concatenate([first[:cut], first[cut:] + via_two.astype(F4)], 0).astype(BF)
        return [own, first, second]

    def square_reduce_end(self, parts, one, two):
        own, first, second = parts
        return own + one(first).astype(F4) + two(second).astype(F4)

    def core_sum(self, keep, send, *earlier):
        other = self.swap_core(send.astype(BF))
        return keep + (after(other, *earlier) if earlier else other).astype(F4)

    def plane_gather(self, own):
        if not self.fast_plane:
            return [(lax.all_gather(own, "seq", axis=0, tiled=True), None, 0)]
        return self.with_core(self.square_gather(own, self.along_x, self.along_y, (2, 4)))

    def plane_reduce(self, keep, send):
        if not self.fast_plane:
            terms = jnp.concatenate([keep, send], 0).astype(BF)
            return lax.psum_scatter(terms, "seq", scatter_dimension=0, tiled=True).astype(F4)
        pair = self.core_sum(keep, send)
        rows = pair.shape[0] // 4
        terms = [pair[i * rows : (i + 1) * rows] for i in range(4)]
        return self.square_reduce(*terms, self.along_x, self.along_y)

    def line_gather(self, own):
        return lax.all_gather(own, "fsdp", axis=0, tiled=True)

    def line_reduce(self, terms):
        return lax.psum_scatter(terms, "fsdp", scatter_dimension=0, tiled=True)

    def swap_blocks(self, blocks):
        return lax.all_to_all(blocks, "seq", split_axis=0, concat_axis=0, tiled=True)

    def rows_sorted(self, blocks):
        return blocks.transpose(1, 0, 2, 3).reshape(-1, blocks.shape[3])

    def rows_by_line(self, rows_in, shard_rows):
        shape = (self.ns, self.nz, shard_rows, rows_in.shape[1])
        return rows_in.reshape(shape).transpose(1, 0, 2, 3)

    def ff_lists(self):
        return [[s * self.nz + f for f in range(self.nz)] for s in range(self.ns)]

    def short_gather_line(self, own):
        held = own[None, :]
        for k in range(1, self.nz):
            other = lax.ppermute(own, "fsdp", [(i, i ^ k) for i in range(self.nz)])
            held = jnp.concatenate([held, other[None, :]], 0)
        bit = 1
        while bit < self.nz:
            pairs = held.reshape(-1, 2, bit, own.shape[0])
            held = jnp.where((self.z & bit) != 0, pairs[:, ::-1], pairs).reshape(held.shape)
            bit *= 2
        return held

    def short_gather_plane(self, held):
        bit = 1
        while bit < self.ns:
            other = self.flip(held, bit)
            high = (self.s & bit) != 0
            first = jnp.where(high, other, held)
            second = jnp.where(high, held, other)
            held = jnp.concatenate([first, second], 0)
            bit *= 2
        return held

    def short_reduce(self, held):
        bit = self.ns // 2
        while bit:
            half = held.shape[0] // 2
            high = (self.s & bit) != 0
            keep = jnp.where(high, held[half:], held[:half])
            send = jnp.where(high, held[:half], held[half:])
            held = keep + self.flip(send, bit)
            bit //= 2
        total = lax.dynamic_index_in_dim(held, self.z, 0, keepdims=False)
        for k in range(1, self.nz):
            send = lax.dynamic_index_in_dim(held, self.z ^ k, 0, keepdims=False)
            total = total + lax.ppermute(send, "fsdp", [(i, i ^ k) for i in range(self.nz)])
        return total


def on_device(
    hidden_in,
    positions,
    norm1_gain,
    norm1_shift,
    w_qkv,
    b_qkv,
    w_out,
    norm2_gain,
    norm2_shift,
    w_gate,
    w_up,
    w_down,
    grad_out,
):
    links = Links()
    ns, nz = links.ns, links.nz
    devices = ns * nz
    tok_rows = hidden_in.shape[1]
    width = hidden_in.shape[2]
    shard_rows = w_qkv.shape[0]
    seq_places = positions[0]
    length = seq_places.shape[0]
    cols = width // ns
    score_scale = HD ** (-0.5)

    lists = links.ff_lists()
    out_here = links.line_gather(w_out)
    short = jnp.concatenate([norm1_gain, norm1_shift, norm2_gain, norm2_shift, b_qkv])
    short_line = links.short_gather_line(short)
    qkv_lists = [[s, ns + s, 2 * ns + s] for s in range(ns)]
    qkv_blocks = links.swap_blocks(pick_columns(w_qkv, qkv_lists))
    qkv_blocks, short_line = turn([qkv_blocks, short_line], out_here)
    qkv_line = links.line_gather(qkv_blocks[None])
    ff_blocks = links.swap_blocks(pair_columns(w_gate, w_up, lists))

    short_all = links.short_gather_plane(short_line)
    short_all, w_down = turn([short_all, w_down])
    n = shard_rows
    first_gain = short_all[:, :n].reshape(-1)
    first_shift = short_all[:, n : 2 * n].reshape(-1)
    second_gain = short_all[:, 2 * n : 3 * n].reshape(-1)
    second_shift = short_all[:, 3 * n : 4 * n].reshape(-1)
    bias_all = short_all[:, 4 * n :].reshape(3, ns, cols)
    bias_here = lax.dynamic_index_in_dim(bias_all, links.s, 1, keepdims=False).reshape(3 * cols)

    place = jnp.stack([links.s, links.z]).astype(jnp.int32)
    order = links.order if links.fast_plane else None
    inputs = hidden_in.reshape(tok_rows, width).astype(F4)
    _, first_hat, first_inverse = layer_norm(inputs, first_gain, first_shift)
    first_pieces = links.plane_gather(hidden_in.reshape(tok_rows, width))
    cotangent_low = grad_out.reshape(tok_rows, width)
    tables = rotary_tables(seq_places, cols)
    half = length // 2

    def let(values, *earlier):
        flat = turn([v for group in values for v in group], *earlier)
        found = []
        for group in values:
            found.append(list(flat[: len(group)]))
            flat = flat[len(group) :]
        return found

    def arrays(pieces):
        return [piece for piece, _, _ in pieces]

    def renewed(pieces, values):
        return [(value, at, start) for value, (_, at, start) in zip(values, pieces)]

    vectors = [v.astype(F4)[None] for v in (first_gain, first_shift, bias_here)]
    found, vectors, (ff_blocks, cotangent_low) = let(
        [arrays(first_pieces), vectors, [ff_blocks, cotangent_low]]
    )
    found, vectors, (cotangent_low,) = let([found, vectors, [cotangent_low]], qkv_line)
    first_pieces = renewed(first_pieces, found)
    ff_line = links.line_gather(ff_blocks[None])
    down_here = links.line_gather(w_down)
    cotangent_pieces = arrays(links.plane_gather(cotangent_low))
    normed_rows, queries, keys, values, mixed, mixed_rel, log_totals = attend(
        place,
        first_pieces,
        vectors[0],
        vectors[1],
        qkv_line,
        vectors[2],
        tables,
        order,
        tok_rows,
    )
    out_send = dot(mixed_rel[half:], out_here, BF)
    out_keep = dot(mixed_rel[:half], out_here)
    middle = inputs + links.plane_reduce(out_keep, out_send)

    second_normed, second_hat, second_inverse = layer_norm(middle, second_gain, second_shift)
    second_low = second_normed.astype(BF)
    second_pieces = arrays(links.plane_gather(second_low))
    second_rows, cotangent_rows, hidden_mid, gate_up = feed(
        second_pieces, cotangent_pieces, ff_line
    )
    down_grad = dot_tn(hidden_mid, cotangent_rows).astype(BF)
    down_sum = links.line_reduce(down_grad)
    grad_rows, gate_up = turn([cotangent_rows, gate_up], down_grad)
    d_ff, second_send, second_keep = feed_back(grad_rows, gate_up, ff_line, down_here)
    ff_grad = links.rows_by_line(dot_tn(second_rows, d_ff).astype(BF), shard_rows)
    ff_sum = links.line_reduce(ff_grad).reshape(ns, shard_rows, -1)
    second_send, second_keep = turn([second_send, second_keep], ff_grad)
    d_second = links.plane_reduce(second_keep, second_send)
    d_second = after(d_second, down_sum)
    d_from_norm, second_gain_grad, second_shift_grad = norm_backward(
        d_second, second_hat, second_inverse, second_gain
    )
    d_middle = cotangent_low.astype(F4) + d_from_norm
    d_middle_pieces = links.plane_gather(d_middle.astype(BF))
    out_grad = outer_rows(mixed_rel, arrays(d_middle_pieces))
    d_middle_rows, d_projected, d_projected_rel, bias_grad = attend_back(
        place,
        d_middle_pieces,
        out_here,
        queries,
        keys,
        values,
        log_totals,
        tables,
        order,
        tok_rows,
    )
    qkv_here = links.rows_sorted(qkv_line)
    first_send = dot_nt(d_projected_rel[half:], qkv_here).astype(BF)
    d_projected = after(d_projected, first_send)
    qkv_grad = links.rows_by_line(dot_tn(normed_rows, d_projected).astype(BF), shard_rows)
    qkv_sum = links.line_reduce(qkv_grad)
    ff_swapped = links.swap_blocks(ff_sum)
    out_share = links.line_reduce(after(out_grad, qkv_sum, ff_swapped))
    qkv_sum = qkv_sum.reshape(ns, shard_rows, -1)
    bias_grad = bias_grad.reshape(3, 1, cols)

    hidden_later = after(hidden_mid, d_middle_rows)
    layer_send = dot(hidden_later[half:], down_here, BF)
    layer_keep = dot(hidden_later[:half], down_here)
    layer_out = (middle + links.plane_reduce(layer_keep, layer_send)).astype(BF)

    first_keep = dot_nt(d_projected_rel[:half], qkv_here)
    d_first = links.plane_reduce(first_keep, first_send)
    d_from_first, first_gain_grad, first_shift_grad = norm_backward(
        d_first, first_hat, first_inverse, first_gain
    )
    grad_in = (d_middle + d_from_first).astype(BF).reshape(1, tok_rows, width)

    placed = lax.dynamic_update_slice(
        jnp.zeros((3, ns, cols), F4), bias_grad, (0, links.s, 0)
    ).reshape(devices, -1)
    short_terms = jnp.concatenate(
        [
            first_gain_grad.reshape(devices, n),
            first_shift_grad.reshape(devices, n),
            second_gain_grad.reshape(devices, n),
            second_shift_grad.reshape(devices, n),
            placed,
        ],
        1,
    )
    short_sums = links.short_reduce(short_terms)

    gate_share, up_share = part_columns(ff_swapped, lists)
    qkv_share = place_columns(links.swap_blocks(qkv_sum), qkv_lists)
    return (
        layer_out.reshape(1, tok_rows, width),
        grad_in,
        short_sums[:n],
        short_sums[n : 2 * n],
        qkv_share,
        short_sums[4 * n :],
        out_share.astype(F4),
        short_sums[2 * n : 3 * n],
        short_sums[3 * n : 4 * n],
        gate_share,
        up_share,
        down_sum.astype(F4),
    )


def solution(mesh):
    both = ("seq", "fsdp")
    rows = P("fsdp", "seq", None)
    vector = P(both)
    matrix = P(both, None)
    return jax.shard_map(
        on_device,
        mesh=mesh,
        in_specs=(
            rows,
            P("fsdp", None),
            vector,
            vector,
            matrix,
            vector,
            matrix,
            vector,
            vector,
            matrix,
            matrix,
            matrix,
            rows,
        ),
        out_specs=(
            rows,
            rows,
            vector,
            vector,
            matrix,
            vector,
            matrix,
            vector,
            vector,
            matrix,
            matrix,
            matrix,
        ),
        check_vma=False,
    )
```

```python
import jax
import jax.numpy as jnp
from jax import lax
from jax.experimental import pallas as pl
from jax.experimental.pallas import tpu as pltpu
from jax.sharding import PartitionSpec as P

HD = 64
ROT = 16

EPS = 1e-05
NEG = -1e30

BF = jnp.bfloat16
F4 = jnp.float32


def dot(a, b, out=F4):
    return jnp.dot(a, b, preferred_element_type=F4).astype(out)


def dot_nt(a, b):
    return lax.dot_general(a, b, (((1,), (1,)), ((), ())), preferred_element_type=F4)


def dot_tn(a, b):
    return lax.dot_general(a, b, (((0,), (0,)), ((), ())), preferred_element_type=F4)


def layer_norm(values, gain_row, shift_row):
    row_mean = jnp.mean(values, axis=1, keepdims=True)
    centred = values - row_mean
    inverse = lax.rsqrt(jnp.mean(centred * centred, axis=1, keepdims=True) + EPS)
    normed = centred * inverse
    return (normed * gain_row.astype(F4) + shift_row.astype(F4), normed, inverse)


def norm_backward(grad_rows, normed, inverse, gain_row):
    scaled = grad_rows * gain_row.astype(F4)
    inner_term = (
        scaled
        - jnp.mean(scaled, axis=1, keepdims=True)
        - normed * jnp.mean(scaled * normed, axis=1, keepdims=True)
    )
    return (inner_term * inverse, jnp.sum(grad_rows * normed, axis=0), jnp.sum(grad_rows, axis=0))


def angle_tables(places):
    half_rot = ROT // 2
    frequency = 10000.0 ** (-2.0 * jnp.arange(half_rot, dtype=F4) / ROT)
    angles = places.astype(F4)[:, None] * frequency[None, :]
    return (
        jnp.concatenate([jnp.cos(angles), jnp.cos(angles)], 1),
        jnp.concatenate([jnp.sin(angles), jnp.sin(angles)], 1),
    )


def busy(microseconds):
    return pl.CostEstimate(
        flops=int(microseconds * 1e9), bytes_accessed=0, transcendentals=0
    )


VMEM_BYTES = 56 << 20
BLOCK = 256


def kernel_dot(a, b, contract):
    return lax.dot_general(a, b, (contract, ((), ())), preferred_element_type=F4)


NN = ((1,), (0,))
NT = ((1,), (1,))


def copy_all(pairs, sems):
    copies = [pltpu.make_async_copy(a, b, sems.at[i]) for i, (a, b) in enumerate(pairs)]
    for copy in copies:
        copy.start()
    for copy in copies:
        copy.wait()


def piece_rows(place, pieces, chunk):
    return [
        0 if at is None else pl.multiple_of((place ^ at) * chunk + start, 16)
        for _, at, start in pieces
    ]


def turned(rows, tables, backward):
    plain, ahead, behind = tables
    width = rows.shape[1]
    half = ROT // 2
    moved = pltpu.roll(rows, width - half, 1) * ahead + pltpu.roll(rows, half, 1) * behind
    return rows * plain - moved if backward else rows * plain + moved


def rotary_tables(places, cols):
    half = ROT // 2
    cosine, sine = angle_tables(places)
    rows = places.shape[0]
    rest = jnp.zeros((rows, HD - ROT), F4)
    none = jnp.zeros((rows, half), F4)
    plain = jnp.concatenate([cosine, rest + 1.0], 1)
    ahead = jnp.concatenate([-sine[:, :half], none, rest], 1)
    behind = jnp.concatenate([none, sine[:, half:], rest], 1)
    return [jnp.tile(table, (1, cols // HD)) for table in (plain, ahead, behind)]


def head_lanes(shape, head):
    return lax.broadcasted_iota(jnp.int32, shape, 1) // HD == head


def attend(place, pieces, gain, shift, qkv_line, bias, tables, order, chunk):
    line, plane, shard, three = qkv_line.shape
    cols = three // 3
    width = line * plane * shard
    length = tables[0].shape[0]
    heads = cols // HD
    count = len(pieces)
    block = min(BLOCK, length)
    score_scale = HD ** (-0.5)

    def kernel(place_ref, *refs):
        piece_refs = refs[:count]
        w_ref, gain_ref, shift_ref, bias_ref, plain_ref, ahead_ref, behind_ref = refs[
            count : count + 7
        ]
        n_ref, q_ref, k_ref, v_ref, o_ref, rel_ref, lse_ref, w_held, sems = refs[count + 7 :]
        here = place_ref[0]
        starts = piece_rows(here, pieces, chunk)
        pairs = [
            (ref, n_ref.at[pl.ds(at, ref.shape[0])]) for ref, at in zip(piece_refs, starts)
        ]
        for f in range(line):
            for s in range(plane):
                pairs.append((w_ref.at[f, s], w_held.at[pl.ds((s * line + f) * shard, shard)]))
        copy_all(pairs, sems)

        def project(i, carry):
            rows = pl.ds(pl.multiple_of(i * block, block), block)
            raw = n_ref[rows, :].astype(F4)
            centred = raw - jnp.mean(raw, axis=1, keepdims=True)
            inverse = lax.rsqrt(jnp.mean(centred * centred, axis=1, keepdims=True) + EPS)
            normed = (centred * inverse * gain_ref[...] + shift_ref[...]).astype(BF)
            n_ref[rows, :] = normed
            found = kernel_dot(normed, w_held[...], NN) + bias_ref[...]
            factors = (plain_ref[rows, :], ahead_ref[rows, :], behind_ref[rows, :])
            q_ref[rows, :] = turned(found[:, :cols], factors, False).astype(BF)
            k_ref[rows, :] = turned(found[:, cols : 2 * cols], factors, False).astype(BF)
            v_ref[rows, :] = found[:, 2 * cols :].astype(BF)
            return carry

        lax.fori_loop(0, length // block, project, 0)
        for i in range(length // block):
            rows = slice(i * block, (i + 1) * block)
            seen = (i + 1) * block
            q_rows = q_ref[rows, :]
            k_rows = k_ref[:seen, :]
            v_rows = v_ref[:seen, :]
            allowed = (
                lax.broadcasted_iota(jnp.int32, (block, seen), 1)
                <= lax.broadcasted_iota(jnp.int32, (block, seen), 0) + i * block
            )
            found = jnp.zeros((block, cols), F4)
            totals = jnp.zeros((block, 128), F4)
            for h in range(heads):
                mine = head_lanes((block, cols), h)
                scores = kernel_dot(jnp.where(mine, q_rows, jnp.zeros_like(q_rows)), k_rows, NT)
                scores = jnp.where(allowed, scores * score_scale, NEG)
                peak = jnp.max(scores, axis=1, keepdims=True)
                weights = jnp.exp(scores - peak)
                total = jnp.sum(weights, axis=1, keepdims=True)
                weights = (weights * (1.0 / total)).astype(BF)
                found = jnp.where(mine, kernel_dot(weights, v_rows, NN), found)
                lane = lax.broadcasted_iota(jnp.int32, (block, 128), 1)
                totals = jnp.where(lane == h, peak + jnp.log(total), totals)
            o_ref[rows, :] = found.astype(BF)
            lse_ref[rows, :] = totals
        if order is None:
            rel_ref[...] = o_ref[...]
        else:
            for k, at in enumerate(order):
                start = pl.multiple_of((here ^ at) * chunk, chunk)
                rel_ref[pl.ds(k * chunk, chunk), :] = o_ref[pl.ds(start, chunk), :]

    anywhere = pl.BlockSpec(memory_space=pl.ANY)
    whole = pl.BlockSpec(memory_space=pltpu.VMEM)
    tall = jax.ShapeDtypeStruct((length, cols), BF)
    return pl.pallas_call(
        kernel,
        out_shape=[
            jax.ShapeDtypeStruct((length, width), BF),
            tall,
            tall,
            tall,
            tall,
            tall,
            jax.ShapeDtypeStruct((length, 128), F4),
        ],
        in_specs=[pl.BlockSpec(memory_space=pltpu.SMEM)] + [anywhere] * (count + 1) + [whole] * 6,
        out_specs=[whole] * 7,
        scratch_shapes=[
            pltpu.VMEM((width, three), BF),
            pltpu.SemaphoreType.DMA((count + line * plane,)),
        ],
        compiler_params=pltpu.CompilerParams(vmem_limit_bytes=VMEM_BYTES),
        cost_estimate=busy(17),
        name="attend",
    )(place, *[piece for piece, _, _ in pieces], qkv_line, gain, shift, bias, *tables)


def attend_back(place, pieces, out_here, q, k, v, lse, tables, order, chunk):
    length, cols = q.shape
    width = out_here.shape[1]
    heads = cols // HD
    count = len(pieces)
    block = min(BLOCK, length)
    score_scale = HD ** (-0.5)

    def kernel(place_ref, *refs):
        piece_refs = refs[:count]
        out_ref, q_ref, k_ref, v_ref, lse_ref, plain_ref, ahead_ref, behind_ref = refs[
            count : count + 8
        ]
        d_ref, all_ref, rel_ref, sum_ref, do_ref, delta_ref, dq_ref, dk_ref, sems = refs[count + 8 :]
        here = place_ref[0]
        starts = piece_rows(here, pieces, chunk)
        copy_all(
            [(ref, d_ref.at[pl.ds(at, ref.shape[0])]) for ref, at in zip(piece_refs, starts)], sems
        )

        def project(i, carry):
            rows = pl.ds(pl.multiple_of(i * block, block), block)
            do_ref[rows, :] = kernel_dot(d_ref[rows, :], out_ref[...], NT).astype(BF)
            return carry

        lax.fori_loop(0, length // block, project, 0)
        for i in range(length // block):
            rows = slice(i * block, (i + 1) * block)
            seen = (i + 1) * block
            q_rows, do_rows = q_ref[rows, :], do_ref[rows, :]
            k_rows, v_rows = k_ref[:seen, :], v_ref[:seen, :]
            allowed = (
                lax.broadcasted_iota(jnp.int32, (block, seen), 1)
                <= lax.broadcasted_iota(jnp.int32, (block, seen), 0) + i * block
            )
            found = jnp.zeros((block, cols), F4)
            deltas = jnp.zeros((block, 128), F4)
            for h in range(heads):
                mine = head_lanes((block, cols), h)
                none = jnp.zeros_like(q_rows)
                scores = kernel_dot(jnp.where(mine, q_rows, none), k_rows, NT) * score_scale
                probs = jnp.where(allowed, jnp.exp(scores - lse_ref[rows, h : h + 1]), 0.0)
                d_probs = kernel_dot(jnp.where(mine, do_rows, none), v_rows, NT)
                delta = jnp.sum(probs * d_probs, axis=1, keepdims=True)
                d_scores = (probs * (d_probs - delta)).astype(BF)
                found = jnp.where(mine, kernel_dot(d_scores, k_rows, NN), found)
                lane = lax.broadcasted_iota(jnp.int32, (block, 128), 1)
                deltas = jnp.where(lane == h, delta, deltas)
            dq_ref[rows, :] = (found * score_scale).astype(BF)
            delta_ref[rows, :] = deltas
        lse_rows = jnp.transpose(lse_ref[...])
        delta_rows = jnp.transpose(delta_ref[...])
        for j in range(length // block):
            rows = slice(j * block, (j + 1) * block)
            left = length - j * block
            k_rows, v_rows = k_ref[rows, :], v_ref[rows, :]
            q_rows, do_rows = q_ref[j * block :, :], do_ref[j * block :, :]
            allowed = lax.broadcasted_iota(jnp.int32, (block, left), 0) <= lax.broadcasted_iota(
                jnp.int32, (block, left), 1
            )
            keys = jnp.zeros((block, cols), F4)
            values = jnp.zeros((block, cols), F4)
            for h in range(heads):
                mine = head_lanes((block, cols), h)
                none = jnp.zeros_like(k_rows)
                scores = kernel_dot(jnp.where(mine, k_rows, none), q_rows, NT) * score_scale
                lse_row = lse_rows[h : h + 1, j * block :]
                probs = jnp.where(allowed, jnp.exp(scores - lse_row), 0.0)
                d_probs = kernel_dot(jnp.where(mine, v_rows, none), do_rows, NT)
                d_scores = (probs * (d_probs - delta_rows[h : h + 1, j * block :])).astype(BF)
                keys = jnp.where(mine, kernel_dot(d_scores, q_rows, NN), keys)
                values = jnp.where(mine, kernel_dot(probs.astype(BF), do_rows, NN), values)
            dk_ref[rows, :] = (keys * score_scale).astype(BF)
            all_ref[rows, 2 * cols :] = values.astype(BF)

        sum_ref[...] = jnp.zeros_like(sum_ref)

        def finish(i, carry):
            rows = pl.ds(pl.multiple_of(i * block, block), block)
            factors = (plain_ref[rows, :], ahead_ref[rows, :], behind_ref[rows, :])
            all_ref[rows, :cols] = turned(dq_ref[rows, :].astype(F4), factors, True).astype(BF)
            all_ref[rows, cols : 2 * cols] = turned(
                dk_ref[rows, :].astype(F4), factors, True
            ).astype(BF)
            sum_ref[...] += jnp.sum(all_ref[rows, :].astype(F4), axis=0, keepdims=True)
            return carry

        lax.fori_loop(0, length // block, finish, 0)
        if order is None:
            rel_ref[...] = all_ref[...]
        else:
            for n, at in enumerate(order):
                start = pl.multiple_of((here ^ at) * chunk, chunk)
                rel_ref[pl.ds(n * chunk, chunk), :] = all_ref[pl.ds(start, chunk), :]

    anywhere = pl.BlockSpec(memory_space=pl.ANY)
    whole = pl.BlockSpec(memory_space=pltpu.VMEM)
    wide = jax.ShapeDtypeStruct((length, 3 * cols), BF)
    return pl.pallas_call(
        kernel,
        out_shape=[
            jax.ShapeDtypeStruct((length, width), BF),
            wide,
            wide,
            jax.ShapeDtypeStruct((1, 3 * cols), F4),
        ],
        in_specs=[pl.BlockSpec(memory_space=pltpu.SMEM)] + [anywhere] * count + [whole] * 8,
        out_specs=[whole] * 4,
        scratch_shapes=[
            pltpu.VMEM((length, cols), BF),
            pltpu.VMEM((length, 128), F4),
            pltpu.VMEM((length, cols), BF),
            pltpu.VMEM((length, cols), BF),
            pltpu.SemaphoreType.DMA((count,)),
        ],
        compiler_params=pltpu.CompilerParams(vmem_limit_bytes=VMEM_BYTES),
        cost_estimate=busy(26),
        name="attend_back",
    )(place, *[piece for piece, _, _ in pieces], out_here, q, k, v, lse, *tables)


def outer_rows(left, pieces):
    count = len(pieces)
    starts, length = [], 0
    for piece in pieces:
        starts.append(length)
        length += piece.shape[0]
    cols, width = left.shape[1], pieces[0].shape[1]

    def kernel(left_ref, *refs):
        held, sems = refs[count + 1 :]
        copy_all(
            [(ref, held.at[pl.ds(at, ref.shape[0])]) for ref, at in zip(refs[:count], starts)], sems
        )
        refs[count][...] = kernel_dot(left_ref[...], held[...], ((0,), (0,))).astype(BF)

    anywhere = pl.BlockSpec(memory_space=pl.ANY)
    whole = pl.BlockSpec(memory_space=pltpu.VMEM)
    return pl.pallas_call(
        kernel,
        out_shape=jax.ShapeDtypeStruct((cols, width), BF),
        in_specs=[whole] + [anywhere] * count,
        out_specs=whole,
        scratch_shapes=[pltpu.VMEM((length, width), BF), pltpu.SemaphoreType.DMA((count,))],
        compiler_params=pltpu.CompilerParams(vmem_limit_bytes=VMEM_BYTES),
        cost_estimate=busy(4),
        name="outer_rows",
    )(left, *pieces)


def feed(pieces, grads, ff_line):
    line, plane, shard, both = ff_line.shape
    cols = both // 2
    width = line * plane * shard
    count = len(pieces)
    starts, length = [], 0
    for piece in pieces:
        starts.append(length)
        length += piece.shape[0]
    block = min(512, length)
    copies = 2 * count + line * plane

    def kernel(*refs):
        piece_refs, grad_refs = refs[:count], refs[count : 2 * count]
        ff_ref = refs[2 * count]
        n_ref, g_ref, a_ref, both_ref, w_held, sems = refs[2 * count + 1 :]
        pairs = []
        for f in range(line):
            for s in range(plane):
                pairs.append((ff_ref.at[f, s], w_held.at[pl.ds((s * line + f) * shard, shard)]))
        for held, found in ((n_ref, piece_refs), (g_ref, grad_refs)):
            for ref, at in zip(found, starts):
                pairs.append((ref, held.at[pl.ds(at, ref.shape[0])]))
        copy_all(pairs, sems)

        def step(i, carry):
            rows = pl.ds(pl.multiple_of(i * block, block), block)
            gate_up = kernel_dot(n_ref[rows, :], w_held[...], NN)
            both_ref[rows, :] = gate_up
            gate, up = gate_up[:, :cols], gate_up[:, cols:]
            a_ref[rows, :] = (gate / (1.0 + jnp.exp(-gate)) * up).astype(BF)
            return carry

        lax.fori_loop(0, length // block, step, 0)

    anywhere = pl.BlockSpec(memory_space=pl.ANY)
    whole = pl.BlockSpec(memory_space=pltpu.VMEM)
    return pl.pallas_call(
        kernel,
        out_shape=[
            jax.ShapeDtypeStruct((length, width), BF),
            jax.ShapeDtypeStruct((length, width), BF),
            jax.ShapeDtypeStruct((length, cols), BF),
            jax.ShapeDtypeStruct((length, both), F4),
        ],
        in_specs=[anywhere] * (2 * count + 1),
        out_specs=[whole] * 4,
        scratch_shapes=[pltpu.VMEM((width, both), BF), pltpu.SemaphoreType.DMA((copies,))],
        compiler_params=pltpu.CompilerParams(vmem_limit_bytes=VMEM_BYTES),
        cost_estimate=busy(17),
        name="feed",
    )(*pieces, *grads, ff_line)


def feed_back(grad_rows, gate_up, ff_line, down_here):
    line, plane, shard, both = ff_line.shape
    cols = both // 2
    length, width = grad_rows.shape
    half = length // 2
    block = min(512, half)

    def kernel(g_ref, both_ref, ff_ref, down_ref, d_ref, send_ref, keep_ref, w_held, sems):
        pairs = []
        for f in range(line):
            for s in range(plane):
                pairs.append((ff_ref.at[f, s], w_held.at[pl.ds((s * line + f) * shard, shard)]))
        copies = [pltpu.make_async_copy(a, b, sems.at[i]) for i, (a, b) in enumerate(pairs)]
        for copy in copies:
            copy.start()

        def step(i, carry):
            rows = pl.ds(pl.multiple_of(i * block, block), block)
            d_hidden = kernel_dot(g_ref[rows, :], down_ref[...], NT)
            gate, up = both_ref[rows, :cols], both_ref[rows, cols:]
            sigmoid = 1.0 / (1.0 + jnp.exp(-gate))
            d_gate = d_hidden * up * sigmoid * (1.0 + gate * (1.0 - sigmoid))
            d_ref[rows, :] = jnp.concatenate([d_gate, d_hidden * gate * sigmoid], 1).astype(BF)
            return carry

        lax.fori_loop(0, length // block, step, 0)
        for copy in copies:
            copy.wait()

        def back(i, carry):
            rows = pl.ds(pl.multiple_of(i * block, block), block)
            there = pl.ds(pl.multiple_of(half + i * block, block), block)
            send_ref[rows, :] = kernel_dot(d_ref[there, :], w_held[...], NT).astype(BF)
            keep_ref[rows, :] = kernel_dot(d_ref[rows, :], w_held[...], NT)
            return carry

        lax.fori_loop(0, half // block, back, 0)

    anywhere = pl.BlockSpec(memory_space=pl.ANY)
    whole = pl.BlockSpec(memory_space=pltpu.VMEM)
    return pl.pallas_call(
        kernel,
        out_shape=[
            jax.ShapeDtypeStruct((length, both), BF),
            jax.ShapeDtypeStruct((half, width), BF),
            jax.ShapeDtypeStruct((half, width), F4),
        ],
        in_specs=[whole, whole, anywhere, whole],
        out_specs=[whole] * 3,
        scratch_shapes=[
            pltpu.VMEM((width, both), BF),
            pltpu.SemaphoreType.DMA((line * plane,)),
        ],
        compiler_params=pltpu.CompilerParams(vmem_limit_bytes=VMEM_BYTES),
        cost_estimate=busy(17),
        name="feed_back",
    )(grad_rows, gate_up, ff_line, down_here)


def nothing(*refs):
    pass


def turn(values, *earlier):
    anywhere = pl.BlockSpec(memory_space=pl.ANY)
    return pl.pallas_call(
        nothing,
        out_shape=[jax.ShapeDtypeStruct(v.shape, v.dtype) for v in values],
        in_specs=[anywhere] * (len(values) + len(earlier)),
        out_specs=[anywhere] * len(values),
        input_output_aliases={i: i for i in range(len(values))},
        cost_estimate=pl.CostEstimate(flops=0, bytes_accessed=0, transcendentals=0),
        name="in_turn",
    )(*values, *earlier)


def after(values, *earlier):
    return turn([values], *earlier)[0]


def pair_columns(gate, up, lists):
    rows, width = gate.shape
    part = width // sum(len(blocks) for blocks in lists)

    def kernel(gate_ref, up_ref, blocks_ref):
        whole = [gate_ref[...].astype(F4), up_ref[...].astype(F4)]
        for i, blocks in enumerate(lists):
            columns = [w[:, at * part : (at + 1) * part] for w in whole for at in blocks]
            blocks_ref[i] = jnp.concatenate(columns, 1).astype(BF)

    held = 2 * part * len(lists[0])
    return pl.pallas_call(
        kernel,
        out_shape=jax.ShapeDtypeStruct((len(lists), rows, held), BF),
        compiler_params=pltpu.CompilerParams(vmem_limit_bytes=32 << 20),
        name="pair_columns",
    )(gate, up)


def part_columns(blocks, lists):
    parts, rows, held = blocks.shape
    count = len(lists[0])
    part = held // (2 * count)
    width = parts * count * part
    place = {at: (i, j) for i, each in enumerate(lists) for j, at in enumerate(each)}

    def kernel(blocks_ref, first_ref, second_ref):
        whole = [blocks_ref[i].astype(F4) for i in range(parts)]
        for k, ref in enumerate((first_ref, second_ref)):
            columns = []
            for at in range(parts * count):
                i, j = place[at]
                start = (k * count + j) * part
                columns.append(whole[i][:, start : start + part])
            ref[...] = jnp.concatenate(columns, 1)

    return pl.pallas_call(
        kernel,
        out_shape=[jax.ShapeDtypeStruct((rows, width), F4)] * 2,
        compiler_params=pltpu.CompilerParams(vmem_limit_bytes=32 << 20),
        name="part_columns",
    )(blocks)


def pick_columns(weight, lists):
    rows, width = weight.shape
    part = width // sum(len(blocks) for blocks in lists)

    def kernel(weight_ref, blocks_ref):
        whole = weight_ref[...].astype(F4)
        for i, blocks in enumerate(lists):
            columns = [whole[:, at * part : (at + 1) * part] for at in blocks]
            blocks_ref[i] = jnp.concatenate(columns, 1).astype(BF)

    return pl.pallas_call(
        kernel,
        out_shape=jax.ShapeDtypeStruct((len(lists), rows, part * len(lists[0])), BF),
        compiler_params=pltpu.CompilerParams(vmem_limit_bytes=32 << 20),
        name="pick_columns",
    )(weight)


def place_columns(blocks, lists):
    parts, rows, held = blocks.shape
    count = len(lists[0])
    part = held // count
    place = {at: (i, j) for i, each in enumerate(lists) for j, at in enumerate(each)}

    def kernel(blocks_ref, whole_ref):
        whole = [blocks_ref[i].astype(F4) for i in range(parts)]
        columns = []
        for at in range(parts * count):
            i, j = place[at]
            columns.append(whole[i][:, j * part : (j + 1) * part])
        whole_ref[...] = jnp.concatenate(columns, 1)

    return pl.pallas_call(
        kernel,
        out_shape=jax.ShapeDtypeStruct((rows, parts * held), F4),
        compiler_params=pltpu.CompilerParams(vmem_limit_bytes=32 << 20),
        name="place_columns",
    )(blocks)


class Links:
    def __init__(self):
        self.ns = lax.axis_size("seq")
        self.nz = lax.axis_size("fsdp")
        self.s = lax.axis_index("seq")
        self.z = lax.axis_index("fsdp")
        self.core = self.s % 2
        self.fast_plane = self.ns == 8
        self.order = [0, 2, 4, 6, 1, 3, 5, 7]

    def flip(self, values, bit):
        return lax.ppermute(values, "seq", [(i, i ^ bit) for i in range(self.ns)])

    def swap_core(self, values):
        return self.flip(values, 1)

    def hop(self, values, pairs):
        return lax.ppermute(values, "fsdp", pairs)

    def along_x(self, values):
        return self.flip(values, 2)

    def along_y(self, values):
        return self.flip(values, 4)

    def square_gather(self, own, one, two, codes):
        cut = own.shape[0] // 32 * 16
        first = one(own)
        second = two(own)
        return [
            (own, 0, 0),
            (first, codes[0], 0),
            (second, codes[1], 0),
            (two(first[:cut]), codes[0] | codes[1], 0),
            (one(second[cut:]), codes[0] | codes[1], cut),
        ]

    def with_core(self, found):
        return found + [(self.swap_core(part), at | 1, start) for part, at, start in found]

    def square_reduce(self, own, first, second, far, one, two):
        return self.square_reduce_end(
            self.square_reduce_start(own, first, second, far, one, two), one, two
        )

    def square_reduce_start(self, own, first, second, far, one, two):
        cut = far.shape[0] // 32 * 16
        far = far.astype(BF)
        via_one = one(far[:cut])
        via_two = two(far[cut:])
        second = jnp.concatenate([second[:cut] + via_one.astype(F4), second[cut:]], 0).astype(BF)
        first = jnp.concatenate([first[:cut], first[cut:] + via_two.astype(F4)], 0).astype(BF)
        return [own, first, second]

    def square_reduce_end(self, parts, one, two):
        own, first, second = parts
        return own + one(first).astype(F4) + two(second).astype(F4)

    def core_sum(self, keep, send, *earlier):
        other = self.swap_core(send.astype(BF))
        return keep + (after(other, *earlier) if earlier else other).astype(F4)

    def plane_gather(self, own):
        if not self.fast_plane:
            return [(lax.all_gather(own, "seq", axis=0, tiled=True), None, 0)]
        return self.with_core(self.square_gather(own, self.along_x, self.along_y, (2, 4)))

    def plane_reduce(self, keep, send):
        if not self.fast_plane:
            terms = jnp.concatenate([keep, send], 0).astype(BF)
            return lax.psum_scatter(terms, "seq", scatter_dimension=0, tiled=True).astype(F4)
        pair = self.core_sum(keep, send)
        rows = pair.shape[0] // 4
        terms = [pair[i * rows : (i + 1) * rows] for i in range(4)]
        return self.square_reduce(*terms, self.along_x, self.along_y)

    def line_gather(self, own):
        return lax.all_gather(own, "fsdp", axis=0, tiled=True)

    def line_reduce(self, terms):
        return lax.psum_scatter(terms, "fsdp", scatter_dimension=0, tiled=True)

    def swap_blocks(self, blocks):
        return lax.all_to_all(blocks, "seq", split_axis=0, concat_axis=0, tiled=True)

    def rows_sorted(self, blocks):
        return blocks.transpose(1, 0, 2, 3).reshape(-1, blocks.shape[3])

    def rows_by_line(self, rows_in, shard_rows):
        shape = (self.ns, self.nz, shard_rows, rows_in.shape[1])
        return rows_in.reshape(shape).transpose(1, 0, 2, 3)

    def ff_lists(self):
        return [[s * self.nz + f for f in range(self.nz)] for s in range(self.ns)]

    def short_gather_line(self, own):
        held = own[None, :]
        for k in range(1, self.nz):
            other = lax.ppermute(own, "fsdp", [(i, i ^ k) for i in range(self.nz)])
            held = jnp.concatenate([held, other[None, :]], 0)
        bit = 1
        while bit < self.nz:
            pairs = held.reshape(-1, 2, bit, own.shape[0])
            held = jnp.where((self.z & bit) != 0, pairs[:, ::-1], pairs).reshape(held.shape)
            bit *= 2
        return held

    def short_gather_plane(self, held):
        bit = 1
        while bit < self.ns:
            other = self.flip(held, bit)
            high = (self.s & bit) != 0
            first = jnp.where(high, other, held)
            second = jnp.where(high, held, other)
            held = jnp.concatenate([first, second], 0)
            bit *= 2
        return held

    def short_reduce(self, held):
        bit = self.ns // 2
        while bit:
            half = held.shape[0] // 2
            high = (self.s & bit) != 0
            keep = jnp.where(high, held[half:], held[:half])
            send = jnp.where(high, held[:half], held[half:])
            held = keep + self.flip(send, bit)
            bit //= 2
        total = lax.dynamic_index_in_dim(held, self.z, 0, keepdims=False)
        for k in range(1, self.nz):
            send = lax.dynamic_index_in_dim(held, self.z ^ k, 0, keepdims=False)
            total = total + lax.ppermute(send, "fsdp", [(i, i ^ k) for i in range(self.nz)])
        return total


def on_device(
    hidden_in,
    positions,
    norm1_gain,
    norm1_shift,
    w_qkv,
    b_qkv,
    w_out,
    norm2_gain,
    norm2_shift,
    w_gate,
    w_up,
    w_down,
    grad_out,
):
    links = Links()
    ns, nz = links.ns, links.nz
    devices = ns * nz
    tok_rows = hidden_in.shape[1]
    width = hidden_in.shape[2]
    shard_rows = w_qkv.shape[0]
    seq_places = positions[0]
    length = seq_places.shape[0]
    cols = width // ns
    score_scale = HD ** (-0.5)

    lists = links.ff_lists()
    out_here = links.line_gather(w_out)
    short = jnp.concatenate([norm1_gain, norm1_shift, norm2_gain, norm2_shift, b_qkv])
    short_line = links.short_gather_line(short)
    qkv_lists = [[s, ns + s, 2 * ns + s] for s in range(ns)]
    qkv_blocks = links.swap_blocks(pick_columns(w_qkv, qkv_lists))
    qkv_blocks, short_line = turn([qkv_blocks, short_line], out_here)
    qkv_line = links.line_gather(qkv_blocks[None])
    ff_blocks = links.swap_blocks(pair_columns(w_gate, w_up, lists))

    short_all = links.short_gather_plane(short_line)
    short_all, w_down = turn([short_all, w_down])
    n = shard_rows
    first_gain = short_all[:, :n].reshape(-1)
    first_shift = short_all[:, n : 2 * n].reshape(-1)
    second_gain = short_all[:, 2 * n : 3 * n].reshape(-1)
    second_shift = short_all[:, 3 * n : 4 * n].reshape(-1)
    bias_all = short_all[:, 4 * n :].reshape(3, ns, cols)
    bias_here = lax.dynamic_index_in_dim(bias_all, links.s, 1, keepdims=False).reshape(3 * cols)

    place = jnp.stack([links.s, links.z]).astype(jnp.int32)
    order = links.order if links.fast_plane else None
    inputs = hidden_in.reshape(tok_rows, width).astype(F4)
    _, first_hat, first_inverse = layer_norm(inputs, first_gain, first_shift)
    first_pieces = links.plane_gather(hidden_in.reshape(tok_rows, width))
    cotangent_low = grad_out.reshape(tok_rows, width)
    tables = rotary_tables(seq_places, cols)
    half = length // 2

    def let(values, *earlier):
        flat = turn([v for group in values for v in group], *earlier)
        found = []
        for group in values:
            found.append(list(flat[: len(group)]))
            flat = flat[len(group) :]
        return found

    def arrays(pieces):
        return [piece for piece, _, _ in pieces]

    def renewed(pieces, values):
        return [(value, at, start) for value, (_, at, start) in zip(values, pieces)]

    vectors = [v.astype(F4)[None] for v in (first_gain, first_shift, bias_here)]
    found, vectors, (ff_blocks,) = let([arrays(first_pieces), vectors, [ff_blocks]])
    found, vectors = let([found, vectors], qkv_line)
    first_pieces = renewed(first_pieces, found)
    ff_line = links.line_gather(ff_blocks[None])
    down_here = links.line_gather(w_down)
    normed_rows, queries, keys, values, mixed, mixed_rel, log_totals = attend(
        place,
        first_pieces,
        vectors[0],
        vectors[1],
        qkv_line,
        vectors[2],
        tables,
        order,
        tok_rows,
    )
    cotangent_pieces = arrays(links.plane_gather(after(cotangent_low, qkv_line)))
    out_send = dot(mixed_rel[half:], out_here, BF)
    out_keep = dot(mixed_rel[:half], out_here)
    middle = inputs + links.plane_reduce(out_keep, out_send)

    second_normed, second_hat, second_inverse = layer_norm(middle, second_gain, second_shift)
    second_low = second_normed.astype(BF)
    second_pieces = arrays(links.plane_gather(second_low))
    second_rows, cotangent_rows, hidden_mid, gate_up = feed(
        second_pieces, cotangent_pieces, ff_line
    )
    down_grad = dot_tn(hidden_mid, cotangent_rows).astype(BF)
    down_sum = links.line_reduce(down_grad)
    grad_rows, gate_up = turn([cotangent_rows, gate_up], down_grad)
    d_ff, second_send, second_keep = feed_back(grad_rows, gate_up, ff_line, down_here)
    ff_grad = links.rows_by_line(dot_tn(second_rows, d_ff).astype(BF), shard_rows)
    ff_sum = links.line_reduce(ff_grad).reshape(ns, shard_rows, -1)
    second_send, second_keep = turn([second_send, second_keep], ff_grad)
    d_second = links.plane_reduce(second_keep, second_send)
    d_second = after(d_second, down_sum)
    d_from_norm, second_gain_grad, second_shift_grad = norm_backward(
        d_second, second_hat, second_inverse, second_gain
    )
    d_middle = cotangent_low.astype(F4) + d_from_norm
    d_middle_pieces = links.plane_gather(d_middle.astype(BF))
    out_grad = outer_rows(mixed_rel, arrays(d_middle_pieces))
    d_middle_rows, d_projected, d_projected_rel, bias_grad = attend_back(
        place,
        d_middle_pieces,
        out_here,
        queries,
        keys,
        values,
        log_totals,
        tables,
        order,
        tok_rows,
    )
    qkv_here = links.rows_sorted(qkv_line)
    first_send = dot_nt(d_projected_rel[half:], qkv_here).astype(BF)
    d_projected = after(d_projected, first_send)
    qkv_grad = links.rows_by_line(dot_tn(normed_rows, d_projected).astype(BF), shard_rows)
    qkv_sum = links.line_reduce(qkv_grad)
    ff_swapped = links.swap_blocks(ff_sum)
    out_share = links.line_reduce(after(out_grad, qkv_sum, ff_swapped))
    qkv_sum = qkv_sum.reshape(ns, shard_rows, -1)
    bias_grad = bias_grad.reshape(3, 1, cols)

    hidden_later = after(hidden_mid, d_middle_rows)
    layer_send = dot(hidden_later[half:], down_here, BF)
    layer_keep = dot(hidden_later[:half], down_here)
    layer_out = (middle + links.plane_reduce(layer_keep, layer_send)).astype(BF)

    first_keep = dot_nt(d_projected_rel[:half], qkv_here)
    d_first = links.plane_reduce(first_keep, first_send)
    d_from_first, first_gain_grad, first_shift_grad = norm_backward(
        d_first, first_hat, first_inverse, first_gain
    )
    grad_in = (d_middle + d_from_first).astype(BF).reshape(1, tok_rows, width)

    placed = lax.dynamic_update_slice(
        jnp.zeros((3, ns, cols), F4), bias_grad, (0, links.s, 0)
    ).reshape(devices, -1)
    short_terms = jnp.concatenate(
        [
            first_gain_grad.reshape(devices, n),
            first_shift_grad.reshape(devices, n),
            second_gain_grad.reshape(devices, n),
            second_shift_grad.reshape(devices, n),
            placed,
        ],
        1,
    )
    short_sums = links.short_reduce(short_terms)

    gate_share, up_share = part_columns(ff_swapped, lists)
    qkv_share = place_columns(links.swap_blocks(qkv_sum), qkv_lists)
    return (
        layer_out.reshape(1, tok_rows, width),
        grad_in,
        short_sums[:n],
        short_sums[n : 2 * n],
        qkv_share,
        short_sums[4 * n :],
        out_share.astype(F4),
        short_sums[2 * n : 3 * n],
        short_sums[3 * n : 4 * n],
        gate_share,
        up_share,
        down_sum.astype(F4),
    )


def solution(mesh):
    both = ("seq", "fsdp")
    rows = P("fsdp", "seq", None)
    vector = P(both)
    matrix = P(both, None)
    return jax.shard_map(
        on_device,
        mesh=mesh,
        in_specs=(
            rows,
            P("fsdp", None),
            vector,
            vector,
            matrix,
            vector,
            matrix,
            vector,
            vector,
            matrix,
            matrix,
            matrix,
            rows,
        ),
        out_specs=(
            rows,
            rows,
            vector,
            vector,
            matrix,
            vector,
            matrix,
            vector,
            vector,
            matrix,
            matrix,
            matrix,
        ),
        check_vma=False,
    )
```
